32 devices in a mesh: ctx: 4 (over z), section: 2 (over x), dp: 4 (over y, core).
Axes of the slice: x: 2, y: 2, z: 4, core: 2. Of those that a mesh axis runs over, the one named last changes fastest.
Arguments:
- query_vectors: bfloat16 [4, 512, 1792], P('dp', 'ctx', 'section'), may hold values from -16 to 16
- key_vectors: bfloat16 [4, 512, 256], P('dp', 'ctx', 'section'), may hold values from -16 to 16
- value_vectors: bfloat16 [4, 512, 256], P('dp', 'ctx', 'section'), may hold values from -6 to 6
- grad_output: bfloat16 [4, 512, 1792], P('dp', 'ctx', 'section'), may hold values from -24 to 24
- output_dots: float32 [4, 14, 512], P('dp', 'section', 'ctx'), may hold values from -12 to 12
- frame_ids: int32 [4, 512], P('dp'), may hold values from 0 to 3, never falling along the last dimension, each value on 1 to 256 neighbouring positions
- visual_rows: int32 [4, 4, 32], P('dp', 'ctx'), may hold values from 0 to 127, as said below
- shuffle_source: int32 [4, 8, 64], P('dp', ('ctx', 'section')), may hold values from 0 to 63, each once within a row
- qkv_weight: bfloat16 [2304, 3584], P(None, ('section', 'dp')), may hold values from -0.125 to 0.125
- projector_weight: bfloat16 [3584, 2560], P(('section', 'dp')), may hold values from -0.09375 to 0.09375
Outputs:
- grad_keys: bfloat16 [4, 512, 256], P('dp', 'ctx', 'section')
- grad_values: bfloat16 [4, 512, 256], P('dp', 'ctx', 'section')
- patch_grads: bfloat16 [4, 512, 640], P('dp', ('ctx', 'section'))
The draws below stay inside these ranges and needn't reach their ends.
Inputs may be any that keep to these rules, and one draw needn't show every extreme that they name: `frame_ids`: frame numbers never fall along a sequence; a frame holds 1 to 256 tokens. `visual_rows`: each block of 128 tokens lists 32 distinct positions in increasing order. `shuffle_source`: each row is a permutation.
All inputs are finite; a program needn't handle non-finite values.
Results may differ from the reference program's by a relative error of at most 0.014.
Values may be sent and summed in bfloat16 or wider, within the bound.
A program may use at most 128 MiB of HBM per device.

```python
import math
import jax
import jax.numpy as jnp
import numpy as np
from jax import lax

D = 3584
HEAD_DIM = 128
GROUP = 7
KV_HEADS = 2
Q_HEADS = 14
SIG_CHAN = 640
TOK_DEV = 128
VIS_DEV = 32
SEQ_LEN = 512
SEQUENCES = 4
FRAME_MAX = 256
FRAME_COUNT = 4
N_CTX = 4


def draw_query_vectors(key, part):
    fresh = jax.random.fold_in(key, 1)
    shape_all = (SEQUENCES, SEQ_LEN, KV_HEADS, GROUP, HEAD_DIM)
    drawn = jnp.clip(1.4 * jax.random.normal(fresh, shape_all, jnp.float32), -8.0, 8.0)
    return drawn.reshape(SEQUENCES, SEQ_LEN, KV_HEADS * GROUP * HEAD_DIM).astype(jnp.bfloat16)


def draw_key_vectors(key, part):
    fresh = jax.random.fold_in(key, 2)
    shape_all = (SEQUENCES, SEQ_LEN, KV_HEADS, HEAD_DIM)
    drawn = jnp.clip(1.4 * jax.random.normal(fresh, shape_all, jnp.float32), -8.0, 8.0)
    return drawn.reshape(SEQUENCES, SEQ_LEN, KV_HEADS * HEAD_DIM).astype(jnp.bfloat16)


def draw_visual_rows(key, part):
    block_total = SEQ_LEN // TOK_DEV
    ranks = jax.random.randint(jax.random.fold_in(key, 3), (SEQUENCES, block_total, TOK_DEV), 0, 1 << 20)
    distinct = ranks * TOK_DEV + jnp.arange(TOK_DEV, dtype=jnp.int32)
    order = jnp.argsort(distinct, axis=-1)[:, :, :VIS_DEV]
    return jnp.sort(order, axis=-1).astype(jnp.int32)


def levels(rng, shape, shards, smallest, top_value):
    level = 1.0
    for axis_at, blocks in shards:
        steps = jax.random.uniform(jax.random.fold_in(jax.random.fold_in(rng, 6), axis_at), (blocks,), jnp.float32, smallest / len(shards), top_value / len(shards))
        level = level * jnp.repeat(jnp.exp(steps), shape[axis_at] // blocks).reshape((-1,) + (1,) * (len(shape) - 1 - axis_at))
    return level


def length_profile(number_of, total, most, lean):
    portions = [(1 << 20) // math.isqrt(standing ** lean) + 1 for standing in range(2, number_of + 1)]
    surplus, holding = total - most - (number_of - 1), [1] * (number_of - 1)
    while surplus > 0:
        movable = [i for i in range(number_of - 1) if holding[i] < most]
        whole, left = sum([portions[i] for i in movable]), surplus
        for i in movable:
            more = min(most - holding[i], max(1, left * portions[i] // whole), surplus)
            holding[i] = holding[i] + more
            surplus = surplus - more
    return np.array([most] + holding)


def uneven_parts(key, amount, total, most, lean):
    if amount == 2:
        one = jax.random.randint(key, (), max(1, total - most), min(most, total - 1) + 1)
        return jnp.stack([one, total - one])
    sizes = jnp.asarray(length_profile(amount, total, most, lean), jnp.int32)
    twos = (amount - 1) // 2
    donor, taker = sizes[1:1 + 2 * twos:2], sizes[2:2 + 2 * twos:2]
    slack = jnp.minimum(donor - 1, most - taker)
    passed = jax.random.randint(jax.random.fold_in(key, 1), (twos,), 0, 1 << 20) % (slack + 1)
    sizes = sizes.at[1:1 + 2 * twos:2].set(donor - passed).at[2:2 + 2 * twos:2].set(taker + passed)
    return sizes[jax.random.permutation(jax.random.fold_in(key, 2), amount)]


def noise(rng, shape, spread, bound, cuts=(), kind=jnp.bfloat16):
    loudness = levels(rng, shape, cuts, -0.22, 0.18) if cuts else 1.0
    values = jax.random.normal(rng, shape, jnp.float32) * spread * loudness
    return jnp.minimum(jnp.maximum(values, -bound), bound).astype(kind)


def setup_inputs(seed: int = 0) -> dict:
    key_list = jax.random.split(jax.random.key(seed), 11)
    query_vectors = draw_query_vectors(jax.random.fold_in(key_list[10], 71), 0)
    key_vectors = draw_key_vectors(jax.random.fold_in(key_list[10], 71), 0)
    value_vectors = noise(key_list[2], (SEQUENCES, SEQ_LEN, KV_HEADS * HEAD_DIM), 1.0, 6.0, ((0, 4), (1, 4), (2, 2)))
    grad_output = noise(key_list[3], (SEQUENCES, SEQ_LEN, Q_HEADS * HEAD_DIM), 4.0, 24.0, ((0, 4), (1, 4), (2, 2)))
    output_dots = noise(key_list[4], (SEQUENCES, Q_HEADS, SEQ_LEN), 2.0, 12.0, ((0, 4), (1, 2), (2, 4)), jnp.float32)
    frame_ids = jax.vmap(lambda own: jnp.searchsorted(jnp.cumsum(uneven_parts(own, FRAME_COUNT, SEQ_LEN, FRAME_MAX, 0)), jnp.arange(SEQ_LEN), side="right"))(jax.random.split(key_list[5], SEQUENCES)).reshape((SEQUENCES, SEQ_LEN)).astype(jnp.int32)
    visual_rows = draw_visual_rows(jax.random.fold_in(key_list[10], 71), 0)
    shuffle_source = jax.vmap(lambda own: jax.random.permutation(own, 2 * VIS_DEV))(jax.random.split(key_list[7], SEQUENCES * (2 * N_CTX))).reshape((SEQUENCES, 2 * N_CTX, 2 * VIS_DEV)).astype(jnp.int32)
    qkv_weight = noise(key_list[8], (KV_HEADS * (GROUP + 2) * HEAD_DIM, D), (KV_HEADS * (GROUP + 2) * HEAD_DIM) ** -0.5, 0.125, ((1, 8),))
    projector_weight = noise(key_list[9], (D, 4 * SIG_CHAN), D ** -0.5, 0.09375, ((0, 8),))
    return dict(query_vectors=query_vectors, key_vectors=key_vectors, value_vectors=value_vectors, grad_output=grad_output, output_dots=output_dots, frame_ids=frame_ids, visual_rows=visual_rows, shuffle_source=shuffle_source, qkv_weight=qkv_weight, projector_weight=projector_weight)


MASKED = -1e+30

def block_mask(frame_line, query_first, key_first, width):
    query_pos = query_first + jnp.arange(width, dtype=jnp.int32)
    key_pos = key_first + jnp.arange(width, dtype=jnp.int32)
    query_frames = lax.dynamic_slice_in_dim(frame_line, query_first, width)
    key_frames = lax.dynamic_slice_in_dim(frame_line, key_first, width)
    allowed = (key_pos[None, :] <= query_pos[:, None]) | (key_frames[None, :] == query_frames[:, None])
    return (allowed, key_frames[0] <= query_frames[width - 1])

def group_backward(query_f, key_f, value_f, grad_f, dots_f, frame_line):
    seq_total = key_f.shape[0]
    width = min(512, seq_total)
    block_count = seq_total // width
    heads_here = query_f.shape[1]
    head_size = query_f.shape[2]
    scale_factor = 1.0 / math.sqrt(head_size)

    def score_block(query_block, key_block):
        return jnp.einsum('qhd,kd->hqk', query_block, key_block, precision=lax.Precision.HIGHEST) * scale_factor

    def statistics(query_index):
        query_first = (query_index * width).astype(jnp.int32)
        query_block = lax.dynamic_slice_in_dim(query_f, query_first, width, 0)

        def visit(key_index, carried):
            key_first = (jnp.asarray(key_index).astype(jnp.int32) * width).astype(jnp.int32)
            allowed, needed = block_mask(frame_line, query_first, key_first, width)

            def update(pair_state):
                running, summed = pair_state
                key_block = lax.dynamic_slice_in_dim(key_f, key_first, width, 0)
                scores = jnp.where(allowed[None], score_block(query_block, key_block), MASKED)
                newest = jnp.maximum(running, scores.max(axis=-1))
                summed = summed * jnp.exp(running - newest) + jnp.exp(scores - newest[:, :, None]).sum(axis=-1)
                return (newest, summed)
            return lax.cond(needed, update, lambda unchanged: unchanged, carried)
        start_pair = (jnp.full((heads_here, width), MASKED, jnp.float32), jnp.zeros((heads_here, width), jnp.float32))
        running, summed = lax.fori_loop(0, block_count, visit, start_pair)
        return running + jnp.log(summed)
    lse_all = lax.map(statistics, jnp.arange(block_count, dtype=jnp.int32))

    def query_step(carried, query_index):
        grad_k, grad_v = carried
        query_first = (query_index * width).astype(jnp.int32)
        query_block = lax.dynamic_slice_in_dim(query_f, query_first, width, 0)
        grad_block = lax.dynamic_slice_in_dim(grad_f, query_first, width, 0)
        dots_block = lax.dynamic_slice_in_dim(dots_f, query_first, width, 1)
        lse_block = lse_all[query_index]

        def visit(key_index, state_now):
            key_first = (jnp.asarray(key_index).astype(jnp.int32) * width).astype(jnp.int32)
            allowed, needed = block_mask(frame_line, query_first, key_first, width)

            def update(inner_state):
                grad_q, grad_keys_now, grad_values_now = inner_state
                key_block = lax.dynamic_slice_in_dim(key_f, key_first, width, 0)
                value_block = lax.dynamic_slice_in_dim(value_f, key_first, width, 0)
                scores = score_block(query_block, key_block)
                probability = jnp.exp(jnp.where(allowed[None], scores - lse_block[:, :, None], MASKED))
                probs_low = lax.optimization_barrier(probability.astype(jnp.bfloat16)).astype(jnp.float32)
                grad_probs = jnp.einsum('qhd,kd->hqk', grad_block, value_block, precision=lax.Precision.HIGHEST)
                grad_scores = lax.optimization_barrier((probability * (grad_probs - dots_block[:, :, None])).astype(jnp.bfloat16)).astype(jnp.float32)
                grad_q = grad_q + jnp.einsum('hqk,kd->qhd', grad_scores, key_block, precision=lax.Precision.HIGHEST) * scale_factor
                key_term = jnp.einsum('hqk,qhd->kd', grad_scores, query_block, precision=lax.Precision.HIGHEST) * scale_factor
                value_term = jnp.einsum('hqk,qhd->kd', probs_low, grad_block, precision=lax.Precision.HIGHEST)
                grad_keys_now = lax.dynamic_update_slice_in_dim(grad_keys_now, lax.dynamic_slice_in_dim(grad_keys_now, key_first, width, 0) + key_term, key_first, 0)
                grad_values_now = lax.dynamic_update_slice_in_dim(grad_values_now, lax.dynamic_slice_in_dim(grad_values_now, key_first, width, 0) + value_term, key_first, 0)
                return (grad_q, grad_keys_now, grad_values_now)
            return lax.cond(needed, update, lambda unchanged: unchanged, state_now)
        zero_query = jnp.zeros((width, heads_here, head_size), jnp.float32)
        grad_q, grad_k, grad_v = lax.fori_loop(0, block_count, visit, (zero_query, grad_k, grad_v))
        return ((grad_k, grad_v), grad_q)
    zero_keys = jnp.zeros((seq_total, head_size), jnp.float32)
    (grad_k, grad_v), grad_q = lax.scan(query_step, (zero_keys, zero_keys), jnp.arange(block_count, dtype=jnp.int32))
    return (grad_q.reshape(seq_total, heads_here, head_size), grad_k, grad_v)

def reference(query_vectors, key_vectors, value_vectors, grad_output, output_dots, frame_ids, visual_rows, shuffle_source, qkv_weight, projector_weight):
    query_all = query_vectors.astype(jnp.float32).reshape(SEQUENCES, SEQ_LEN, KV_HEADS, GROUP, HEAD_DIM)
    grad_all = grad_output.astype(jnp.float32).reshape(SEQUENCES, SEQ_LEN, KV_HEADS, GROUP, HEAD_DIM)
    key_all = key_vectors.astype(jnp.float32).reshape(SEQUENCES, SEQ_LEN, KV_HEADS, HEAD_DIM)
    value_all = value_vectors.astype(jnp.float32).reshape(SEQUENCES, SEQ_LEN, KV_HEADS, HEAD_DIM)
    dots_all = output_dots.reshape(SEQUENCES, KV_HEADS, GROUP, SEQ_LEN)
    key_grads = []
    value_grads = []
    patch_list = []
    for seq_index in range(SEQUENCES):
        query_parts = []
        key_parts = []
        value_parts = []
        for head_group in range(KV_HEADS):
            grad_q, grad_k, grad_v = group_backward(query_all[seq_index, :, head_group], key_all[seq_index, :, head_group], value_all[seq_index, :, head_group], grad_all[seq_index, :, head_group], dots_all[seq_index, head_group], frame_ids[seq_index])
            query_parts.append(grad_q.astype(jnp.bfloat16).reshape(SEQ_LEN, GROUP * HEAD_DIM))
            key_parts.append(grad_k.astype(jnp.bfloat16))
            value_parts.append(grad_v.astype(jnp.bfloat16))
        positions = (jnp.arange(N_CTX, dtype=jnp.int32)[:, None] * TOK_DEV + visual_rows[seq_index].astype(jnp.int32)).reshape(-1)
        picked = jnp.concatenate([jnp.concatenate([query_parts[head_group][positions], key_parts[head_group][positions], value_parts[head_group][positions]], axis=1) for head_group in range(KV_HEADS)], axis=1)
        visual_grad = jnp.dot(picked, qkv_weight, preferred_element_type=jnp.float32).astype(jnp.bfloat16)
        shuffled = jnp.dot(visual_grad, projector_weight, preferred_element_type=jnp.float32)
        slot_rows = shuffled.reshape(N_CTX * 2, VIS_DEV // 2 * 4, SIG_CHAN)
        patches = jnp.take_along_axis(slot_rows, shuffle_source[seq_index][:, :, None], axis=1)
        patch_list.append(patches.reshape(N_CTX * 4 * VIS_DEV, SIG_CHAN).astype(jnp.bfloat16))
        key_grads.append(jnp.stack(key_parts, axis=1).reshape(SEQ_LEN, KV_HEADS * HEAD_DIM))
        value_grads.append(jnp.stack(value_parts, axis=1).reshape(SEQ_LEN, KV_HEADS * HEAD_DIM))
    return (jnp.stack(key_grads), jnp.stack(value_grads), jnp.stack(patch_list))
```

```python
import functools
import math

import jax
import jax.numpy as jnp
from jax import lax
from jax.experimental import pallas as pl
from jax.experimental.pallas import tpu as pltpu
from jax.sharding import PartitionSpec as P

HEAD = 128
GROUP = 7
MASKED = -1e30
MESH = pl.DeviceIdType.MESH
CHUNKS = 2
BF = jnp.bfloat16
F32 = jnp.float32


def dot(a, b, over=(1, 0)):
    return lax.dot_general(a, b, (((over[0],), (over[1],)), ((), ())), preferred_element_type=F32)


def kernel(
    n, sections, replicas,
    q_in, k_in, v_in, g_in, dots, frames, rows, source, wq_in, wp_in,
    dk_out, dv_out, patch_out,
    qs, gs, kbuf, vbuf, sbuf, gsend, grecv, wq, wp, top, total, gq_acc, gqsel, kvsel, psend, precv,
    load_sem, k_send, k_recv, v_send, v_recv, g_send, g_recv, a_send, a_recv, b_send, b_recv, p_send, p_recv,
):
    me = lax.axis_index("ctx")
    sec = lax.axis_index("section")
    rep = lax.axis_index("dp")
    tok = k_in.shape[1]
    vis = rows.shape[2]
    half = vis // 2
    width = GROUP * HEAD
    scale = 1.0 / math.sqrt(HEAD)
    factor = scale * math.log2(math.e)
    plane = [(a, b) for a in range(sections) for b in range(replicas) if a or b]

    def each(low, high, body):
        if n <= 8:
            for at in range(low, high):
                body(at)
        else:
            lax.fori_loop(low, high, lambda at, c: (body(at), c)[1], 0)

    def ahead(o):
        return {"ctx": lax.rem(me + o, n)}

    def behind(o):
        return {"ctx": lax.rem(me - o + n, n)}

    def peer(a, b):
        return {"section": lax.rem(sec + a, sections), "dp": lax.rem(rep + b, replicas)}

    def peer_back(a, b):
        return {"section": lax.rem(sec + a, sections), "dp": lax.rem(rep - b + replicas, replicas)}

    barrier = pltpu.get_barrier_semaphore()
    each(1, n, lambda o: pl.semaphore_signal(barrier, inc=1, device_id=ahead(o), device_id_type=MESH))
    for a, b in plane:
        pl.semaphore_signal(barrier, inc=1, device_id=peer(a, b), device_id_type=MESH)

    loads = [
        pltpu.make_async_copy(k_in.at[0], kbuf.at[0], load_sem.at[0]),
        pltpu.make_async_copy(v_in.at[0], vbuf.at[0], load_sem.at[1]),
        pltpu.make_async_copy(wq_in, wq, load_sem.at[2]),
        pltpu.make_async_copy(wp_in, wp, load_sem.at[3]),
    ]
    q_loads = [
        pltpu.make_async_copy(
            q_in.at[0, :, pl.ds(h * HEAD, HEAD)], qs.at[pl.ds(h * HEAD, HEAD), :], load_sem.at[4 + h]
        )
        for h in range(GROUP)
    ]
    g_loads = [
        pltpu.make_async_copy(
            g_in.at[0, :, pl.ds(h * HEAD, HEAD)], gs.at[pl.ds(h * HEAD, HEAD), :], load_sem.at[4 + GROUP + h]
        )
        for h in range(GROUP)
    ]
    loads[0].start()
    for c in q_loads:
        c.start()
    loads[1].start()
    for c in g_loads:
        c.start()
    loads[2].start()
    loads[3].start()
    pl.semaphore_wait(barrier, (n - 1) + len(plane))

    def remote(src, dst, send, recv, device):
        return pltpu.make_async_remote_copy(
            src_ref=src, dst_ref=dst, send_sem=send, recv_sem=recv, device_id=device, device_id_type=MESH
        )

    def k_copy(o):
        return remote(k_in.at[0], kbuf.at[o], k_send.at[o], k_recv.at[o], ahead(o))

    def v_copy(o):
        return remote(v_in.at[0], vbuf.at[o], v_send.at[o], v_recv.at[o], ahead(o))

    def g_copy(o):
        return remote(gsend.at[o], grecv.at[o], g_send.at[o], g_recv.at[o], behind(o))

    def sel_copy(buf, send, recv, a, b):
        return remote(
            buf.at[0, pl.ds(0, vis)], buf.at[a, pl.ds(b * vis, vis)], send.at[a, b], recv.at[a, b], peer(a, b)
        )

    columns = wp.shape[1] // CHUNKS

    def p_copy(i, a, b):
        first = b * vis + lax.rem(sec + a, sections) * half
        return remote(
            psend.at[i, pl.ds(pl.multiple_of(first, half), half)],
            precv.at[i, a, b],
            p_send.at[i, a, b],
            p_recv.at[i, a, b],
            peer_back(a, b),
        )

    each(1, n, lambda o: k_copy(o).start())
    each(1, n, lambda o: v_copy(o).start())

    query_frames = frames[:, pl.ds(pl.multiple_of(me * tok, tok), tok)]
    row_at = lax.broadcasted_iota(jnp.int32, (tok, tok), 0)
    col_at = lax.broadcasted_iota(jnp.int32, (tok, tok), 1)
    hot_t = (lax.broadcasted_iota(jnp.int32, (tok, vis), 0) == rows[0]).astype(F32).astype(BF)
    eye = (row_at == col_at).astype(F32).astype(BF)
    hot = dot(hot_t, eye, (0, 0)).astype(BF)
    dots_row = jnp.concatenate([dots[0, h : h + 1, :] for h in range(GROUP)], axis=1)

    def bias_for(o):
        first = lax.rem(me - o + n, n) * tok
        line = frames[:, pl.ds(pl.multiple_of(first, tok), tok)].astype(F32)
        key_frames = jnp.transpose(jnp.broadcast_to(line, (tok, tok)))
        allowed = (first + row_at <= me * tok + col_at) | (key_frames == query_frames.astype(F32))
        bias = jnp.where(allowed, 0.0, MASKED)
        return jnp.concatenate([bias] * GROUP, axis=1)

    top[...] = jnp.full_like(top, MASKED)
    total[...] = jnp.zeros_like(total)
    gq_acc[...] = jnp.zeros_like(gq_acc)

    def first_pass(o):
        s = dot(kbuf[o], qs[...], (1, 1)) + bias_for(o)
        sbuf[o] = s
        top[...] = jnp.maximum(top[...], jnp.max(s, axis=0, keepdims=True))

    def first_remote(o):
        k_copy(o).wait_recv()
        first_pass(o)

    loads[0].wait()
    for c in q_loads:
        c.wait()
    first_pass(0)
    each(1, n, first_remote)

    def second_pass(o):
        e = jnp.exp2((sbuf[o] - top[...]) * factor)
        sbuf[o] = e
        total[...] += jnp.sum(e, axis=0, keepdims=True)

    each(0, n, second_pass)
    total[...] = 1.0 / total[...]

    loads[1].wait()
    for c in g_loads:
        c.wait()

    def third_pass(o):
        p = sbuf[o] * total[...]
        gp = dot(vbuf[o], gs[...], (1, 1))
        gsc = (p * (gp - dots_row)).astype(BF)
        gv = dot(p.astype(BF), gs[...])
        gk = dot(gsc, qs[...]) * scale
        gq_acc[...] += dot(kbuf[o], gsc, (0, 0))
        return gk, gv

    def third_remote(o):
        v_copy(o).wait_recv()
        gk, gv = third_pass(o)
        gsend[o, 0] = gk.astype(BF)
        gsend[o, 1] = gv.astype(BF)
        g_copy(o).start()

    each(1, n, third_remote)
    gk, gv = third_pass(0)

    gq = (gq_acc[...] * scale).astype(BF)
    for h in range(GROUP):
        gqsel[0, 0:vis, h * HEAD : (h + 1) * HEAD] = dot(
            hot, gq[:, h * HEAD : (h + 1) * HEAD], (1, 1)
        ).astype(BF)
    for a, b in plane:
        sel_copy(gqsel, a_send, a_recv, a, b).start()

    if n <= 8:
        for o in range(1, n):
            g_copy(o).wait_recv()
            gk = gk + grecv[o, 0].astype(F32)
            gv = gv + grecv[o, 1].astype(F32)
    else:

        def gather(o, pair):
            g_copy(o).wait_recv()
            return pair[0] + grecv[o, 0].astype(F32), pair[1] + grecv[o, 1].astype(F32)

        gk, gv = lax.fori_loop(1, n, gather, (gk, gv))
    gk, gv = gk.astype(BF), gv.astype(BF)
    kvsel[0, 0:vis, 0:HEAD] = dot(hot, gk).astype(BF)
    kvsel[0, 0:vis, HEAD : 2 * HEAD] = dot(hot, gv).astype(BF)
    for a, b in plane:
        sel_copy(kvsel, b_send, b_recv, a, b).start()
    dk_out[0] = gk
    dv_out[0] = gv

    loads[2].wait()
    loads[3].wait()
    part = width + 2 * HEAD
    for a, b in plane:
        sel_copy(gqsel, a_send, a_recv, a, b).wait_recv()

    def weight_rows(a, offset, size):
        first = lax.rem(sec - a + sections, sections) * part + offset
        return wq[pl.ds(pl.multiple_of(first, HEAD), size), :]

    grad = dot(gqsel[0], weight_rows(0, 0, width))
    for a in range(1, sections):
        grad = grad + dot(gqsel[a], weight_rows(a, 0, width))
    for a, b in plane:
        sel_copy(kvsel, b_send, b_recv, a, b).wait_recv()
    for a in range(sections):
        grad = grad + dot(kvsel[a], weight_rows(a, width, 2 * HEAD))
    grad = grad.astype(BF)

    for i in range(CHUNKS):
        psend[i] = dot(grad, wp[:, i * columns : (i + 1) * columns]).astype(BF)
        for a, b in plane:
            p_copy(i, a, b).start()

    slots = source.shape[2]
    quarter = wp.shape[1] // 4
    at = lax.broadcasted_iota(jnp.int32, (slots, slots), 0)
    slot_of = lax.rem(at, half) * 4 + lax.div(at, half)
    moved_t = (slot_of == source[0]).astype(F32).astype(BF)

    pieces = []
    for i in range(CHUNKS):
        mine = psend[i, pl.ds(pl.multiple_of(sec * half, half), half), :].astype(F32)
        for a, b in plane:
            p_copy(i, a, b).wait_recv()
            mine = mine + precv[i, a, b].astype(F32)
        for c in range(columns // quarter):
            pieces.append(mine[:, c * quarter : (c + 1) * quarter])
    merged = jnp.concatenate(pieces, axis=0).astype(BF)
    patch_out[0] = dot(moved_t, merged, (0, 0)).astype(BF)

    each(1, n, lambda o: k_copy(o).wait_send())
    each(1, n, lambda o: v_copy(o).wait_send())
    each(1, n, lambda o: g_copy(o).wait_send())
    for a, b in plane:
        sel_copy(gqsel, a_send, a_recv, a, b).wait_send()
        sel_copy(kvsel, b_send, b_recv, a, b).wait_send()
        for i in range(CHUNKS):
            p_copy(i, a, b).wait_send()


def solution(mesh):
    n, sections, replicas = mesh.shape["ctx"], mesh.shape["section"], mesh.shape["dp"]

    def shards(q, k, v, g, dots, frames, rows, source, wq, wp):
        tok, vis = k.shape[1], rows.shape[2]
        half = vis // 2
        width = GROUP * HEAD
        slots, quarter = source.shape[2], wp.shape[1] // 4
        anywhere = pl.BlockSpec(memory_space=pl.ANY)
        inside = pl.BlockSpec(memory_space=pltpu.VMEM)
        dma = pltpu.SemaphoreType.DMA
        return pl.pallas_call(
            functools.partial(kernel, n, sections, replicas),
            out_shape=(
                jax.ShapeDtypeStruct(k.shape, BF),
                jax.ShapeDtypeStruct(v.shape, BF),
                jax.ShapeDtypeStruct((1, slots, quarter), BF),
            ),
            in_specs=[anywhere] * 4 + [inside] * 4 + [anywhere] * 2,
            out_specs=(inside, inside, inside),
            scratch_shapes=[
                pltpu.VMEM((width, HEAD), BF),
                pltpu.VMEM((width, HEAD), BF),
                pltpu.VMEM((n, tok, HEAD), BF),
                pltpu.VMEM((n, tok, HEAD), BF),
                pltpu.VMEM((n, tok, width), F32),
                pltpu.VMEM((n, 2, tok, HEAD), BF),
                pltpu.VMEM((n, 2, tok, HEAD), BF),
                pltpu.VMEM(wq.shape, BF),
                pltpu.VMEM(wp.shape, BF),
                pltpu.VMEM((1, width), F32),
                pltpu.VMEM((1, width), F32),
                pltpu.VMEM((HEAD, width), F32),
                pltpu.VMEM((sections, replicas * vis, width), BF),
                pltpu.VMEM((sections, replicas * vis, 2 * HEAD), BF),
                pltpu.VMEM((CHUNKS, replicas * vis, wp.shape[1] // CHUNKS), BF),
                pltpu.VMEM((CHUNKS, sections, replicas, half, wp.shape[1] // CHUNKS), BF),
                dma((4 + 2 * GROUP,)),
                dma((n,)), dma((n,)), dma((n,)), dma((n,)), dma((n,)), dma((n,)),
                dma((sections, replicas)), dma((sections, replicas)),
                dma((sections, replicas)), dma((sections, replicas)),
                dma((CHUNKS, sections, replicas)), dma((CHUNKS, sections, replicas)),
            ],
            compiler_params=pltpu.CompilerParams(
                collective_id=0, has_side_effects=True, vmem_limit_bytes=56 * 1024 * 1024
            ),
        )(q, k, v, g, dots, frames, rows, source, wq, wp)

    placed = (
        P("dp", "ctx", "section"),
        P("dp", "ctx", "section"),
        P("dp", "ctx", "section"),
        P("dp", "ctx", "section"),
        P("dp", "section", "ctx"),
        P("dp", None),
        P("dp", "ctx", None),
        P("dp", ("ctx", "section"), None),
        P(None, ("section", "dp")),
        P(("section", "dp"), None),
    )
    return jax.shard_map(
        shards,
        mesh=mesh,
        in_specs=placed,
        out_specs=(
            P("dp", "ctx", "section"),
            P("dp", "ctx", "section"),
            P("dp", ("ctx", "section"), None),
        ),
        check_vma=False,
    )
```

```python
import functools
import math

import jax
import jax.numpy as jnp
from jax import lax
from jax.experimental import pallas as pl
from jax.experimental.pallas import tpu as pltpu
from jax.sharding import PartitionSpec as P

HEAD = 128
GROUP = 7
MASKED = -1e30
MESH = pl.DeviceIdType.MESH
CHUNKS = 2
BF = jnp.bfloat16
F32 = jnp.float32


def dot(a, b, over=(1, 0)):
    return lax.dot_general(a, b, (((over[0],), (over[1],)), ((), ())), preferred_element_type=F32)


def kernel(
    n, sections, replicas,
    q_in, k_in, v_in, g_in, dots, frames, rows, source, wq_in, wp_in,
    dk_out, dv_out, patch_out,
    qs, gs, qst, gst, kbuf, vbuf, sbuf, gsend, grecv, wq, wp, swapped, top, total, gq_acc, gqsel, kvsel, gradbuf, psend, precv,
    load_sem, k_send, k_recv, v_send, v_recv, g_send, g_recv, a_send, a_recv, b_send, b_recv, p_send, p_recv, w_send, w_recv, s_send, s_recv,
):
    me = lax.axis_index("ctx")
    sec = lax.axis_index("section")
    rep = lax.axis_index("dp")
    tok = k_in.shape[1]
    vis = rows.shape[2]
    half = vis // 2
    width = GROUP * HEAD
    scale = 1.0 / math.sqrt(HEAD)
    factor = scale * math.log2(math.e)
    plane = [(a, b) for a in range(sections) for b in range(replicas) if a or b]

    def each(low, high, body):
        if n <= 8:
            for at in range(low, high):
                body(at)
        else:
            lax.fori_loop(low, high, lambda at, c: (body(at), c)[1], 0)

    def ahead(o):
        return {"ctx": lax.rem(me + o, n)}

    def behind(o):
        return {"ctx": lax.rem(me - o + n, n)}

    def peer(a, b):
        return {"section": lax.rem(sec + a, sections), "dp": lax.rem(rep + b, replicas)}

    def peer_back(a, b):
        return {"section": lax.rem(sec + a, sections), "dp": lax.rem(rep - b + replicas, replicas)}

    core = lax.rem(rep, 2)
    partner = {"dp": rep + 1 - 2 * core}
    columns = wp.shape[1] // CHUNKS

    def half_columns(which):
        return pl.ds(pl.multiple_of(which * wp.shape[1], wp.shape[1]), wp.shape[1])

    barrier = pltpu.get_barrier_semaphore()
    each(1, n, lambda o: pl.semaphore_signal(barrier, inc=1, device_id=ahead(o), device_id_type=MESH))
    for a, b in plane:
        pl.semaphore_signal(barrier, inc=1, device_id=peer(a, b), device_id_type=MESH)

    loads = [
        pltpu.make_async_copy(k_in.at[0], kbuf.at[0], load_sem.at[0]),
        pltpu.make_async_copy(v_in.at[0], vbuf.at[0], load_sem.at[1]),
        pltpu.make_async_copy(wq_in, wq, load_sem.at[2]),
        pltpu.make_async_copy(wp_in.at[:, half_columns(core)], wp, load_sem.at[3]),
    ]
    q_loads = [
        pltpu.make_async_copy(
            q_in.at[0, :, pl.ds(h * HEAD, HEAD)], qs.at[pl.ds(h * HEAD, HEAD), :], load_sem.at[4 + h]
        )
        for h in range(GROUP)
    ]
    g_loads = [
        pltpu.make_async_copy(
            g_in.at[0, :, pl.ds(h * HEAD, HEAD)], gs.at[pl.ds(h * HEAD, HEAD), :], load_sem.at[4 + GROUP + h]
        )
        for h in range(GROUP)
    ]
    loads[0].start()
    for c in q_loads:
        c.start()
    loads[1].start()
    for c in g_loads:
        c.start()
    loads[2].start()
    loads[3].start()
    pl.semaphore_wait(barrier, (n - 1) + len(plane))

    def remote(src, dst, send, recv, device):
        return pltpu.make_async_remote_copy(
            src_ref=src, dst_ref=dst, send_sem=send, recv_sem=recv, device_id=device, device_id_type=MESH
        )

    def k_copy(o):
        return remote(k_in.at[0], kbuf.at[o], k_send.at[o], k_recv.at[o], ahead(o))

    def v_copy(o):
        return remote(v_in.at[0], vbuf.at[o], v_send.at[o], v_recv.at[o], ahead(o))

    def g_copy(o):
        return remote(gsend.at[o], grecv.at[o], g_send.at[o], g_recv.at[o], behind(o))

    mine_at = pl.ds(pl.multiple_of(rep * vis, vis), vis)

    def sel_copy(buf, send, recv, a, b):
        return remote(buf.at[0, mine_at], buf.at[a, mine_at], send.at[a, b], recv.at[a, b], peer(a, b))

    def weight_copy():
        return remote(wp_in.at[:, half_columns(1 - core)], swapped, w_send.at[0], w_recv.at[0], partner)

    def grad_copy():
        return remote(gradbuf.at[0], gradbuf.at[1], s_send.at[0], s_recv.at[0], partner)

    def p_copy(i, a, b):
        first = lax.rem(rep - b + replicas, replicas) * vis + lax.rem(sec + a, sections) * half
        return remote(
            psend.at[i, pl.ds(pl.multiple_of(first, half), half)],
            precv.at[i, a, b],
            p_send.at[i, a, b],
            p_recv.at[i, a, b],
            peer_back(a, b),
        )

    each(1, n, lambda o: k_copy(o).start())
    each(1, n, lambda o: v_copy(o).start())
    weight_copy().start()

    query_frames = frames[:, pl.ds(pl.multiple_of(me * tok, tok), tok)]
    row_at = lax.broadcasted_iota(jnp.int32, (tok, tok), 0)
    col_at = lax.broadcasted_iota(jnp.int32, (tok, tok), 1)
    hot_t = (lax.broadcasted_iota(jnp.int32, (tok, vis), 0) == rows[0]).astype(F32).astype(BF)
    eye = (row_at == col_at).astype(F32).astype(BF)
    hot = dot(hot_t, eye, (0, 0)).astype(BF)
    dots_row = jnp.concatenate([dots[h] for h in range(GROUP)], axis=1)

    def bias_for(o):
        first = lax.rem(me - o + n, n) * tok
        line = frames[:, pl.ds(pl.multiple_of(first, tok), tok)].astype(F32)
        key_frames = jnp.transpose(jnp.broadcast_to(line, (tok, tok)))
        allowed = (first + row_at <= me * tok + col_at) | (key_frames == query_frames.astype(F32))
        bias = jnp.where(allowed, 0.0, MASKED)
        return jnp.concatenate([bias] * GROUP, axis=1)

    top[...] = jnp.full_like(top, MASKED)
    total[...] = jnp.zeros_like(total)
    gq_acc[...] = jnp.zeros_like(gq_acc)

    def first_pass(o):
        s = dot(kbuf[o], qst[...]) + bias_for(o)
        sbuf[o] = s
        top[...] = jnp.maximum(top[...], jnp.max(s, axis=0, keepdims=True))

    def first_remote(o):
        k_copy(o).wait_recv()
        first_pass(o)

    loads[0].wait()
    for h, c in enumerate(q_loads):
        c.wait()
        at = pl.ds(h * HEAD, HEAD)
        qst[:, at] = jnp.transpose(qs[at, :])
    first_pass(0)
    for h, c in enumerate(g_loads):
        c.wait()
        at = pl.ds(h * HEAD, HEAD)
        gst[:, at] = jnp.transpose(gs[at, :])
    each(1, n, first_remote)

    def second_pass(o):
        e = jnp.exp2((sbuf[o] - top[...]) * factor)
        sbuf[o] = e
        total[...] += jnp.sum(e, axis=0, keepdims=True)

    each(0, n, second_pass)
    total[...] = 1.0 / total[...]

    loads[1].wait()

    def third_pass(o):
        p = sbuf[o] * total[...]
        gp = dot(vbuf[o], gst[...])
        gsc = (p * (gp - dots_row)).astype(BF)
        gv = dot(p.astype(BF), gs[...])
        gk = dot(gsc, qs[...]) * scale
        gq_acc[...] += dot(kbuf[o], gsc, (0, 0))
        return gk, gv

    def third_remote(at):
        o = (at + n // 2 - 1) % (n - 1) + 1
        v_copy(o).wait_recv()
        gk, gv = third_pass(o)
        gsend[o, 0] = gk.astype(BF)
        gsend[o, 1] = gv.astype(BF)
        g_copy(o).start()

    each(0, n - 1, third_remote)
    gk, gv = third_pass(0)

    gq = (gq_acc[...] * scale).astype(BF)
    for h in range(GROUP):
        gqsel[0, mine_at, h * HEAD : (h + 1) * HEAD] = dot(
            hot, gq[:, h * HEAD : (h + 1) * HEAD], (1, 1)
        ).astype(BF)
    for a, b in plane:
        sel_copy(gqsel, a_send, a_recv, a, b).start()

    if n <= 8:
        for o in range(1, n):
            g_copy(o).wait_recv()
            gk = gk + grecv[o, 0].astype(F32)
            gv = gv + grecv[o, 1].astype(F32)
    else:

        def gather(o, pair):
            g_copy(o).wait_recv()
            return pair[0] + grecv[o, 0].astype(F32), pair[1] + grecv[o, 1].astype(F32)

        gk, gv = lax.fori_loop(1, n, gather, (gk, gv))
    gk, gv = gk.astype(BF), gv.astype(BF)
    kvsel[0, mine_at, 0:HEAD] = dot(hot, gk).astype(BF)
    kvsel[0, mine_at, HEAD : 2 * HEAD] = dot(hot, gv).astype(BF)
    for a, b in plane:
        sel_copy(kvsel, b_send, b_recv, a, b).start()
    dk_out[0] = gk
    dv_out[0] = gv

    loads[2].wait()
    loads[3].wait()
    part = width + 2 * HEAD
    for a, b in plane:
        sel_copy(gqsel, a_send, a_recv, a, b).wait_recv()

    def weight_rows(a, offset, size):
        first = lax.rem(sec - a + sections, sections) * part + offset
        return wq[:, pl.ds(pl.multiple_of(first, HEAD), size)]

    grad = dot(weight_rows(0, 0, width), gqsel[0], (1, 1))
    for a in range(1, sections):
        grad = grad + dot(weight_rows(a, 0, width), gqsel[a], (1, 1))
    for a, b in plane:
        sel_copy(kvsel, b_send, b_recv, a, b).wait_recv()
    for a in range(sections):
        grad = grad + dot(weight_rows(a, width, 2 * HEAD), kvsel[a], (1, 1))
    gradbuf[0] = grad.astype(BF)
    grad_copy().start()
    own = dot(gradbuf[0], wp[...], (0, 0))
    weight_copy().wait_recv()
    grad_copy().wait_recv()
    other = jnp.transpose(gradbuf[1])
    for i in range(CHUNKS):
        at = slice(i * columns, (i + 1) * columns)
        psend[i] = (own[:, at] + dot(other, swapped[:, at])).astype(BF)
        for a, b in plane:
            p_copy(i, a, b).start()

    slots = source.shape[2]
    at = lax.broadcasted_iota(jnp.int32, (slots, slots), 0)
    slot_of = lax.rem(at, half) * 4 + lax.div(at, half)
    moved_t = (slot_of == source[0]).astype(F32).astype(BF)

    near, far = [], []
    for i in range(CHUNKS):
        even = psend[i, pl.ds(pl.multiple_of(rep * vis + sec * half, half), half), :].astype(F32)
        odd = jnp.zeros_like(even)
        for a, b in plane:
            p_copy(i, a, b).wait_recv()
            if b % 2:
                odd = odd + precv[i, a, b].astype(F32)
            else:
                even = even + precv[i, a, b].astype(F32)
        near.append(even)
        far.append(odd)
    first = [jnp.where(core == 0, x, y) for x, y in zip(near, far)]
    second = [jnp.where(core == 0, y, x) for x, y in zip(near, far)]
    pieces = first + second
    merged = jnp.concatenate(pieces, axis=0).astype(BF)
    patch_out[0] = dot(moved_t, merged, (0, 0)).astype(BF)

    each(1, n, lambda o: k_copy(o).wait_send())
    each(1, n, lambda o: v_copy(o).wait_send())
    each(1, n, lambda o: g_copy(o).wait_send())
    weight_copy().wait_send()
    grad_copy().wait_send()
    for a, b in plane:
        sel_copy(gqsel, a_send, a_recv, a, b).wait_send()
        sel_copy(kvsel, b_send, b_recv, a, b).wait_send()
        for i in range(CHUNKS):
            p_copy(i, a, b).wait_send()


def hand_on(a, b, c, a_out, b_out, c_out, sems):
    copies = [
        pltpu.make_async_copy(x, y, sems.at[i]) for i, (x, y) in enumerate(((a, a_out), (b, b_out), (c, c_out)))
    ]
    for copy in copies:
        copy.start()
    for copy in copies:
        copy.wait()


def solution(mesh):
    n, sections, replicas = mesh.shape["ctx"], mesh.shape["section"], mesh.shape["dp"]

    def shards(q, k, v, g, dots, frames, rows, source, wq, wp):
        tok, vis = k.shape[1], rows.shape[2]
        half = vis // 2
        width = GROUP * HEAD
        slots, quarter = source.shape[2], wp.shape[1] // 4
        anywhere = pl.BlockSpec(memory_space=pl.ANY)
        inside = pl.BlockSpec(memory_space=pltpu.VMEM)
        dma = pltpu.SemaphoreType.DMA
        model, side = wp.shape[0], wp.shape[1] // 2
        shapes = (
            jax.ShapeDtypeStruct(k.shape, BF),
            jax.ShapeDtypeStruct(v.shape, BF),
            jax.ShapeDtypeStruct((1, slots, quarter), BF),
        )
        outs = pl.pallas_call(
            functools.partial(kernel, n, sections, replicas),
            out_shape=shapes,
            in_specs=[anywhere] * 4 + [inside] * 4 + [anywhere] * 2,
            out_specs=(inside, inside, inside),
            scratch_shapes=[
                pltpu.VMEM((width, HEAD), BF),
                pltpu.VMEM((width, HEAD), BF),
                pltpu.VMEM((HEAD, width), BF),
                pltpu.VMEM((HEAD, width), BF),
                pltpu.VMEM((n, tok, HEAD), BF),
                pltpu.VMEM((n, tok, HEAD), BF),
                pltpu.VMEM((n, tok, width), F32),
                pltpu.VMEM((n, 2, tok, HEAD), BF),
                pltpu.VMEM((n, 2, tok, HEAD), BF),
                pltpu.VMEM((model, wq.shape[0]), BF),
                pltpu.VMEM((model, side), BF),
                pltpu.VMEM((model, side), BF),
                pltpu.VMEM((1, width), F32),
                pltpu.VMEM((1, width), F32),
                pltpu.VMEM((HEAD, width), F32),
                pltpu.VMEM((sections, replicas * vis, width), BF),
                pltpu.VMEM((sections, replicas * vis, 2 * HEAD), BF),
                pltpu.VMEM((2, model, replicas * vis), BF),
                pltpu.VMEM((CHUNKS, replicas * vis, side // CHUNKS), BF),
                pltpu.VMEM((CHUNKS, sections, replicas, half, side // CHUNKS), BF),
                dma((4 + 2 * GROUP,)),
                dma((n,)), dma((n,)), dma((n,)), dma((n,)), dma((n,)), dma((n,)),
                dma((sections, replicas)), dma((sections, replicas)),
                dma((sections, replicas)), dma((sections, replicas)),
                dma((CHUNKS, sections, replicas)), dma((CHUNKS, sections, replicas)),
                dma((1,)), dma((1,)), dma((1,)), dma((1,)),
            ],
            compiler_params=pltpu.CompilerParams(
                collective_id=0, has_side_effects=True, vmem_limit_bytes=56 * 1024 * 1024
            ),
        )(q, k, v, g, dots.transpose(1, 0, 2), frames, rows, source, wq.T, wp)
        return pl.pallas_call(
            hand_on,
            out_shape=shapes,
            in_specs=[pl.BlockSpec(memory_space=pltpu.HBM)] * 3,
            out_specs=(pl.BlockSpec(memory_space=pltpu.HBM),) * 3,
            scratch_shapes=[dma((3,))],
        )(*outs)

    placed = (
        P("dp", "ctx", "section"),
        P("dp", "ctx", "section"),
        P("dp", "ctx", "section"),
        P("dp", "ctx", "section"),
        P("dp", "section", "ctx"),
        P("dp", None),
        P("dp", "ctx", None),
        P("dp", ("ctx", "section"), None),
        P(None, ("section", "dp")),
        P(("section", "dp"), None),
    )
    return jax.shard_map(
        shards,
        mesh=mesh,
        in_specs=placed,
        out_specs=(
            P("dp", "ctx", "section"),
            P("dp", "ctx", "section"),
            P("dp", ("ctx", "section"), None),
        ),
        check_vma=False,
    )
```

```python
import functools
import math

import jax
import jax.numpy as jnp
from jax import lax
from jax.experimental import pallas as pl
from jax.experimental.pallas import tpu as pltpu
from jax.sharding import PartitionSpec as P

HEAD = 128
GROUP = 7
MASKED = -1e30
MESH = pl.DeviceIdType.MESH
CHUNKS = 2
BF = jnp.bfloat16
F32 = jnp.float32


def dot(a, b, over=(1, 0)):
    return lax.dot_general(a, b, (((over[0],), (over[1],)), ((), ())), preferred_element_type=F32)


def kernel(
    n, sections, replicas,
    q_in, k_in, v_in, g_in, dots, frames, rows, source, wq_in, wp_in,
    dk_out, dv_out, patch_out,
    qs, gs, qst, gst, kbuf, vbuf, sbuf, gsend, grecv, hots, rsend, rrecv, wq, wp, swapped, top, total, gq_acc, gqsel, kvsel, gradbuf, psend, precv,
    load_sem, k_send, k_recv, v_send, v_recv, g_send, g_recv, a_send, a_recv, b_send, b_recv, p_send, p_recv, w_send, w_recv, s_send, s_recv, h_send, h_recv, r_send, r_recv,
):
    me = lax.axis_index("ctx")
    sec = lax.axis_index("section")
    rep = lax.axis_index("dp")
    tok = k_in.shape[1]
    vis = rows.shape[2]
    half = vis // 2
    width = GROUP * HEAD
    scale = 1.0 / math.sqrt(HEAD)
    factor = scale * math.log2(math.e)
    plane = [(a, b) for a in range(sections) for b in range(replicas) if a or b]

    def each(low, high, body):
        if n <= 8:
            for at in range(low, high):
                body(at)
        else:
            lax.fori_loop(low, high, lambda at, c: (body(at), c)[1], 0)

    def ahead(o):
        return {"ctx": lax.rem(me + o, n)}

    def behind(o):
        return {"ctx": lax.rem(me - o + n, n)}

    def peer(a, b):
        return {"section": lax.rem(sec + a, sections), "dp": lax.rem(rep + b, replicas)}

    def peer_back(a, b):
        return {"section": lax.rem(sec + a, sections), "dp": lax.rem(rep - b + replicas, replicas)}

    core = lax.rem(rep, 2)
    partner = {"dp": rep + 1 - 2 * core}
    columns = wp.shape[1] // CHUNKS

    def half_columns(which):
        return pl.ds(pl.multiple_of(which * wp.shape[1], wp.shape[1]), wp.shape[1])

    barrier = pltpu.get_barrier_semaphore()
    each(1, n, lambda o: pl.semaphore_signal(barrier, inc=1, device_id=ahead(o), device_id_type=MESH))
    for a, b in plane:
        pl.semaphore_signal(barrier, inc=1, device_id=peer(a, b), device_id_type=MESH)

    loads = [
        pltpu.make_async_copy(k_in.at[0], kbuf.at[0], load_sem.at[0]),
        pltpu.make_async_copy(v_in.at[0], vbuf.at[0], load_sem.at[1]),
        pltpu.make_async_copy(wq_in, wq, load_sem.at[2]),
        pltpu.make_async_copy(wp_in.at[:, half_columns(core)], wp, load_sem.at[3]),
    ]
    q_loads = [
        pltpu.make_async_copy(
            q_in.at[0, :, pl.ds(h * HEAD, HEAD)], qs.at[pl.ds(h * HEAD, HEAD), :], load_sem.at[4 + h]
        )
        for h in range(GROUP)
    ]
    g_loads = [
        pltpu.make_async_copy(
            g_in.at[0, :, pl.ds(h * HEAD, HEAD)], gs.at[pl.ds(h * HEAD, HEAD), :], load_sem.at[4 + GROUP + h]
        )
        for h in range(GROUP)
    ]
    loads[0].start()
    for c in q_loads:
        c.start()
    loads[1].start()
    for c in g_loads:
        c.start()
    loads[2].start()
    loads[3].start()
    pl.semaphore_wait(barrier, (n - 1) + len(plane))

    def remote(src, dst, send, recv, device):
        return pltpu.make_async_remote_copy(
            src_ref=src, dst_ref=dst, send_sem=send, recv_sem=recv, device_id=device, device_id_type=MESH
        )

    def k_copy(o):
        return remote(k_in.at[0], kbuf.at[o], k_send.at[o], k_recv.at[o], ahead(o))

    def v_copy(o):
        return remote(v_in.at[0], vbuf.at[o], v_send.at[o], v_recv.at[o], ahead(o))

    def g_copy(o):
        return remote(gsend.at[o], grecv.at[o], g_send.at[o], g_recv.at[o], behind(o))

    def h_copy(o):
        return remote(hots.at[0], hots.at[o], h_send.at[o], h_recv.at[o], ahead(o))

    def r_copy(o):
        return remote(rsend.at[o], rrecv.at[o], r_send.at[o], r_recv.at[o], behind(o))

    def pass_copy(a, b):
        at = pl.ds(pl.multiple_of(lax.rem(rep - b + replicas, replicas) * vis, vis), vis)
        return remote(gqsel.at[a, at], gqsel.at[a, at], a_send.at[a, b + 1], a_recv.at[a, b + 1], partner)

    across = [(a, b) for a, b in plane if b % 2 == 0]
    mine_at = pl.ds(pl.multiple_of(rep * vis, vis), vis)

    def sel_copy(buf, send, recv, a, b):
        return remote(buf.at[0, mine_at], buf.at[a, mine_at], send.at[a, b], recv.at[a, b], peer(a, b))

    def weight_copy():
        return remote(wp_in.at[:, half_columns(1 - core)], swapped, w_send.at[0], w_recv.at[0], partner)

    def grad_copy():
        return remote(gradbuf.at[0], gradbuf.at[1], s_send.at[0], s_recv.at[0], partner)

    def p_copy(i, a, b):
        first = lax.rem(rep - b + replicas, replicas) * vis + lax.rem(sec + a, sections) * half
        return remote(
            psend.at[i, pl.ds(pl.multiple_of(first, half), half)],
            precv.at[i, a, b],
            p_send.at[i, a, b],
            p_recv.at[i, a, b],
            peer_back(a, b),
        )

    each(1, n, lambda o: k_copy(o).start())
    each(1, n, lambda o: v_copy(o).start())
    weight_copy().start()

    query_frames = frames[:, pl.ds(pl.multiple_of(me * tok, tok), tok)]
    row_at = lax.broadcasted_iota(jnp.int32, (tok, tok), 0)
    col_at = lax.broadcasted_iota(jnp.int32, (tok, tok), 1)
    hot_t = (lax.broadcasted_iota(jnp.int32, (tok, vis), 0) == rows[0]).astype(F32).astype(BF)
    eye = (row_at == col_at).astype(F32).astype(BF)
    hot = dot(hot_t, eye, (0, 0)).astype(BF)
    hots[0] = hot
    each(1, n, lambda o: h_copy(o).start())
    dots_row = jnp.concatenate([dots[h] for h in range(GROUP)], axis=1)

    def bias_for(o):
        first = lax.rem(me - o + n, n) * tok
        line = frames[:, pl.ds(pl.multiple_of(first, tok), tok)].astype(F32)
        key_frames = jnp.transpose(jnp.broadcast_to(line, (tok, tok)))
        allowed = (first + row_at <= me * tok + col_at) | (key_frames == query_frames.astype(F32))
        bias = jnp.where(allowed, 0.0, MASKED)
        return jnp.concatenate([bias] * GROUP, axis=1)

    top[...] = jnp.full_like(top, MASKED)
    total[...] = jnp.zeros_like(total)
    gq_acc[...] = jnp.zeros_like(gq_acc)

    def first_pass(o):
        s = dot(kbuf[o], qst[...]) + bias_for(o)
        sbuf[o] = s
        top[...] = jnp.maximum(top[...], jnp.max(s, axis=0, keepdims=True))

    def first_remote(o):
        k_copy(o).wait_recv()
        first_pass(o)

    loads[0].wait()
    for h, c in enumerate(q_loads):
        c.wait()
        at = pl.ds(h * HEAD, HEAD)
        qst[:, at] = jnp.transpose(qs[at, :])
    first_pass(0)
    for h, c in enumerate(g_loads):
        c.wait()
        at = pl.ds(h * HEAD, HEAD)
        gst[:, at] = jnp.transpose(gs[at, :])
    each(1, n, first_remote)

    def second_pass(o):
        e = jnp.exp2((sbuf[o] - top[...]) * factor)
        sbuf[o] = e
        total[...] += jnp.sum(e, axis=0, keepdims=True)

    each(0, n, second_pass)
    total[...] = 1.0 / total[...]

    loads[1].wait()

    def third_pass(o):
        p = sbuf[o] * total[...]
        gp = dot(vbuf[o], gst[...])
        gsc = (p * (gp - dots_row)).astype(BF)
        gv = dot(p.astype(BF), gs[...])
        gk = dot(gsc, qs[...]) * scale
        gq_acc[...] += dot(kbuf[o], gsc, (0, 0))
        return gk, gv

    def third_remote(at):
        o = (at + n // 2 - 1) % (n - 1) + 1
        v_copy(o).wait_recv()
        h_copy(o).wait_recv()
        gk, gv = third_pass(o)
        gk, gv = gk.astype(BF), gv.astype(BF)
        gsend[o, 0] = gk
        gsend[o, 1] = gv
        rsend[o, :, 0:HEAD] = dot(hots[o], gk).astype(BF)
        rsend[o, :, HEAD : 2 * HEAD] = dot(hots[o], gv).astype(BF)
        r_copy(o).start()

    each(0, n - 1, third_remote)
    gk, gv = third_pass(0)

    gq = (gq_acc[...] * scale).astype(BF)
    for h in range(GROUP):
        gqsel[0, mine_at, h * HEAD : (h + 1) * HEAD] = dot(
            hot, gq[:, h * HEAD : (h + 1) * HEAD], (1, 1)
        ).astype(BF)
    for a, b in across:
        sel_copy(gqsel, a_send, a_recv, a, b).start()
    pass_copy(0, 0).start()
    each(1, n, lambda o: g_copy(o).start())

    def picked(x):
        return lax.dot_general(
            hot.astype(F32), x, (((1,), (0,)), ((), ())),
            precision=lax.Precision.HIGHEST, preferred_element_type=F32,
        )

    def gather(copy, read, start):
        def step(o, pair):
            copy(o).wait_recv()
            x, y = read(o)
            return pair[0] + x.astype(F32), pair[1] + y.astype(F32)

        if n <= 8:
            for o in range(1, n):
                start = step(o, start)
            return start
        return lax.fori_loop(1, n, step, start)

    rows_k, rows_v = gather(
        r_copy, lambda o: (rrecv[o, :, 0:HEAD], rrecv[o, :, HEAD : 2 * HEAD]), (picked(gk), picked(gv))
    )
    kvsel[0, mine_at, 0:HEAD] = rows_k.astype(BF)
    kvsel[0, mine_at, HEAD : 2 * HEAD] = rows_v.astype(BF)
    for a, b in plane:
        sel_copy(kvsel, b_send, b_recv, a, b).start()
    for a, b in across:
        sel_copy(gqsel, a_send, a_recv, a, b).wait_recv()
        pass_copy(a, b).start()

    loads[2].wait()
    loads[3].wait()
    part = width + 2 * HEAD
    for a, b in [(0, 0)] + across:
        pass_copy(a, b).wait_recv()

    def weight_rows(a, offset, size):
        first = lax.rem(sec - a + sections, sections) * part + offset
        return wq[:, pl.ds(pl.multiple_of(first, HEAD), size)]

    grad = dot(weight_rows(0, 0, width), gqsel[0], (1, 1))
    for a in range(1, sections):
        grad = grad + dot(weight_rows(a, 0, width), gqsel[a], (1, 1))
    for a, b in plane:
        sel_copy(kvsel, b_send, b_recv, a, b).wait_recv()
    for a in range(sections):
        grad = grad + dot(weight_rows(a, width, 2 * HEAD), kvsel[a], (1, 1))
    gradbuf[0] = grad.astype(BF)
    grad_copy().start()
    own = dot(gradbuf[0], wp[...], (0, 0))
    weight_copy().wait_recv()
    grad_copy().wait_recv()
    other = jnp.transpose(gradbuf[1])
    for i in range(CHUNKS):
        at = slice(i * columns, (i + 1) * columns)
        psend[i] = (own[:, at] + dot(other, swapped[:, at])).astype(BF)
        for a, b in plane:
            p_copy(i, a, b).start()

    gk, gv = gather(g_copy, lambda o: (grecv[o, 0], grecv[o, 1]), (gk, gv))
    dk_out[0] = gk.astype(BF)
    dv_out[0] = gv.astype(BF)

    slots = source.shape[2]
    at = lax.broadcasted_iota(jnp.int32, (slots, slots), 0)
    slot_of = lax.rem(at, half) * 4 + lax.div(at, half)
    moved_t = (slot_of == source[0]).astype(F32).astype(BF)

    near, far = [], []
    for i in range(CHUNKS):
        even = psend[i, pl.ds(pl.multiple_of(rep * vis + sec * half, half), half), :].astype(F32)
        odd = jnp.zeros_like(even)
        for a, b in plane:
            p_copy(i, a, b).wait_recv()
            if b % 2:
                odd = odd + precv[i, a, b].astype(F32)
            else:
                even = even + precv[i, a, b].astype(F32)
        near.append(even)
        far.append(odd)
    first = [jnp.where(core == 0, x, y) for x, y in zip(near, far)]
    second = [jnp.where(core == 0, y, x) for x, y in zip(near, far)]
    pieces = first + second
    merged = jnp.concatenate(pieces, axis=0).astype(BF)
    patch_out[0] = dot(moved_t, merged, (0, 0)).astype(BF)

    each(1, n, lambda o: k_copy(o).wait_send())
    each(1, n, lambda o: v_copy(o).wait_send())
    each(1, n, lambda o: g_copy(o).wait_send())
    each(1, n, lambda o: h_copy(o).wait_send())
    each(1, n, lambda o: r_copy(o).wait_send())
    pass_copy(0, 0).wait_send()
    for a, b in across:
        sel_copy(gqsel, a_send, a_recv, a, b).wait_send()
        pass_copy(a, b).wait_send()
    weight_copy().wait_send()
    grad_copy().wait_send()
    for a, b in plane:
        sel_copy(kvsel, b_send, b_recv, a, b).wait_send()
        for i in range(CHUNKS):
            p_copy(i, a, b).wait_send()


def hand_on(a, b, c, a_out, b_out, c_out):
    a_out[...] = a[...]
    b_out[...] = b[...]
    c_out[...] = c[...]


def solution(mesh):
    n, sections, replicas = mesh.shape["ctx"], mesh.shape["section"], mesh.shape["dp"]

    def shards(q, k, v, g, dots, frames, rows, source, wq, wp):
        tok, vis = k.shape[1], rows.shape[2]
        half = vis // 2
        width = GROUP * HEAD
        slots, quarter = source.shape[2], wp.shape[1] // 4
        anywhere = pl.BlockSpec(memory_space=pl.ANY)
        inside = pl.BlockSpec(memory_space=pltpu.VMEM)
        dma = pltpu.SemaphoreType.DMA
        model, side = wp.shape[0], wp.shape[1] // 2
        shapes = (
            jax.ShapeDtypeStruct(k.shape, BF),
            jax.ShapeDtypeStruct(v.shape, BF),
            jax.ShapeDtypeStruct((1, slots, quarter), BF),
        )
        outs = pl.pallas_call(
            functools.partial(kernel, n, sections, replicas),
            out_shape=shapes,
            in_specs=[anywhere] * 4 + [inside] * 4 + [anywhere] * 2,
            out_specs=(inside, inside, inside),
            scratch_shapes=[
                pltpu.VMEM((width, HEAD), BF),
                pltpu.VMEM((width, HEAD), BF),
                pltpu.VMEM((HEAD, width), BF),
                pltpu.VMEM((HEAD, width), BF),
                pltpu.VMEM((n, tok, HEAD), BF),
                pltpu.VMEM((n, tok, HEAD), BF),
                pltpu.VMEM((n, tok, width), F32),
                pltpu.VMEM((n, 2, tok, HEAD), BF),
                pltpu.VMEM((n, 2, tok, HEAD), BF),
                pltpu.VMEM((n, vis, tok), BF),
                pltpu.VMEM((n, vis, 2 * HEAD), BF),
                pltpu.VMEM((n, vis, 2 * HEAD), BF),
                pltpu.VMEM((model, wq.shape[0]), BF),
                pltpu.VMEM((model, side), BF),
                pltpu.VMEM((model, side), BF),
                pltpu.VMEM((1, width), F32),
                pltpu.VMEM((1, width), F32),
                pltpu.VMEM((HEAD, width), F32),
                pltpu.VMEM((sections, replicas * vis, width), BF),
                pltpu.VMEM((sections, replicas * vis, 2 * HEAD), BF),
                pltpu.VMEM((2, model, replicas * vis), BF),
                pltpu.VMEM((CHUNKS, replicas * vis, side // CHUNKS), BF),
                pltpu.VMEM((CHUNKS, sections, replicas, half, side // CHUNKS), BF),
                dma((4 + 2 * GROUP,)),
                dma((n,)), dma((n,)), dma((n,)), dma((n,)), dma((n,)), dma((n,)),
                dma((sections, replicas)), dma((sections, replicas)),
                dma((sections, replicas)), dma((sections, replicas)),
                dma((CHUNKS, sections, replicas)), dma((CHUNKS, sections, replicas)),
                dma((1,)), dma((1,)), dma((1,)), dma((1,)),
                dma((n,)), dma((n,)), dma((n,)), dma((n,)),
            ],
            compiler_params=pltpu.CompilerParams(
                collective_id=0, has_side_effects=True, vmem_limit_bytes=56 * 1024 * 1024
            ),
        )(q, k, v, g, dots.transpose(1, 0, 2), frames, rows, source, wq.T, wp)
        return pl.pallas_call(
            hand_on,
            out_shape=shapes,
            in_specs=[inside] * 3,
            out_specs=(inside,) * 3,
        )(*outs)

    placed = (
        P("dp", "ctx", "section"),
        P("dp", "ctx", "section"),
        P("dp", "ctx", "section"),
        P("dp", "ctx", "section"),
        P("dp", "section", "ctx"),
        P("dp", None),
        P("dp", "ctx", None),
        P("dp", ("ctx", "section"), None),
        P(None, ("section", "dp")),
        P(("section", "dp"), None),
    )
    return jax.shard_map(
        shards,
        mesh=mesh,
        in_specs=placed,
        out_specs=(
            P("dp", "ctx", "section"),
            P("dp", "ctx", "section"),
            P("dp", ("ctx", "section"), None),
        ),
        check_vma=False,
    )
```

```python
import functools
import math

import jax
import jax.numpy as jnp
from jax import lax
from jax.experimental import pallas as pl
from jax.experimental.pallas import tpu as pltpu
from jax.sharding import PartitionSpec as P

HEAD = 128
GROUP = 7
MASKED = -1e30
MESH = pl.DeviceIdType.MESH
CHUNKS = 2
BF = jnp.bfloat16
F32 = jnp.float32


def dot(a, b, over=(1, 0)):
    return lax.dot_general(a, b, (((over[0],), (over[1],)), ((), ())), preferred_element_type=F32)


def kernel(
    n, sections, replicas,
    q_in, k_in, v_in, g_in, dots_in, frames_in, rows_in, source_in, wq_in, wp_in,
    dk_out, dv_out, patch_out,
    dots, frames, rows, source, qs, gs, qst, gst, kbuf, vbuf, sbuf, gsend, grecv, hots, rsend, rrecv, wq, wp, swapped, top, total, gq_acc, gqsel, kvsel, gradbuf, psend, precv,
    load_sem, k_send, k_recv, v_send, v_recv, g_send, g_recv, a_send, a_recv, b_send, b_recv, p_send, p_recv, w_send, w_recv, s_send, s_recv, h_send, h_recv, r_send, r_recv,
):
    me = lax.axis_index("ctx")
    sec = lax.axis_index("section")
    rep = lax.axis_index("dp")
    tok = k_in.shape[1]
    vis = rows.shape[2]
    unrolled = n <= 8
    half = vis // 2
    width = GROUP * HEAD
    scale = 1.0 / math.sqrt(HEAD)
    factor = scale * math.log2(math.e)
    plane = [(a, b) for a in range(sections) for b in range(replicas) if a or b]

    def each(low, high, body):
        if n <= 8:
            for at in range(low, high):
                body(at)
        else:
            lax.fori_loop(low, high, lambda at, c: (body(at), c)[1], 0)

    def ahead(o):
        return {"ctx": lax.rem(me + o, n)}

    def behind(o):
        return {"ctx": lax.rem(me - o + n, n)}

    def peer(a, b):
        return {"section": lax.rem(sec + a, sections), "dp": lax.rem(rep + b, replicas)}

    def peer_back(a, b):
        return {"section": lax.rem(sec + a, sections), "dp": lax.rem(rep - b + replicas, replicas)}

    core = lax.rem(rep, 2)
    partner = {"dp": rep + 1 - 2 * core}
    columns = wp.shape[1] // CHUNKS

    def half_columns(which):
        return pl.ds(pl.multiple_of(which * wp.shape[1], wp.shape[1]), wp.shape[1])

    barrier = pltpu.get_barrier_semaphore()
    each(1, n, lambda o: pl.semaphore_signal(barrier, inc=1, device_id=ahead(o), device_id_type=MESH))
    for a, b in plane:
        pl.semaphore_signal(barrier, inc=1, device_id=peer(a, b), device_id_type=MESH)

    loads = [
        pltpu.make_async_copy(k_in.at[0], kbuf.at[0], load_sem.at[0]),
        pltpu.make_async_copy(v_in.at[0], vbuf.at[0], load_sem.at[1]),
        pltpu.make_async_copy(wq_in, wq, load_sem.at[2]),
        pltpu.make_async_copy(wp_in.at[:, half_columns(core)], wp, load_sem.at[3]),
    ]
    q_loads = [
        pltpu.make_async_copy(
            q_in.at[0, :, pl.ds(h * HEAD, HEAD)], qs.at[pl.ds(h * HEAD, HEAD), :], load_sem.at[4 + h]
        )
        for h in range(GROUP)
    ]
    g_loads = [
        pltpu.make_async_copy(
            g_in.at[0, :, pl.ds(h * HEAD, HEAD)], gs.at[pl.ds(h * HEAD, HEAD), :], load_sem.at[4 + GROUP + h]
        )
        for h in range(GROUP)
    ]
    small = [
        pltpu.make_async_copy(x, y, load_sem.at[4 + 2 * GROUP + i])
        for i, (x, y) in enumerate(((frames_in, frames), (rows_in, rows), (dots_in, dots), (source_in, source)))
    ]
    loads[0].start()
    for c in small:
        c.start()
    for c in q_loads:
        c.start()
    loads[1].start()
    for c in g_loads:
        c.start()
    loads[2].start()
    loads[3].start()
    pl.semaphore_wait(barrier, (n - 1) + len(plane))

    def remote(src, dst, send, recv, device):
        return pltpu.make_async_remote_copy(
            src_ref=src, dst_ref=dst, send_sem=send, recv_sem=recv, device_id=device, device_id_type=MESH
        )

    def k_copy(o):
        return remote(k_in.at[0], kbuf.at[o], k_send.at[o], k_recv.at[o], ahead(o))

    def v_copy(o):
        return remote(v_in.at[0], vbuf.at[o], v_send.at[o], v_recv.at[o], ahead(o))

    def g_copy(o):
        return remote(gsend.at[o], grecv.at[o], g_send.at[o], g_recv.at[o], behind(o))

    def h_copy(o):
        return remote(hots.at[0], hots.at[o], h_send.at[o], h_recv.at[o], ahead(o))

    def r_copy(o):
        return remote(rsend.at[o], rrecv.at[o], r_send.at[o], r_recv.at[o], behind(o))

    def pass_copy(a, b):
        at = pl.ds(pl.multiple_of(lax.rem(rep - b + replicas, replicas) * vis, vis), vis)
        return remote(gqsel.at[a, at], gqsel.at[a, at], a_send.at[a, b + 1], a_recv.at[a, b + 1], partner)

    across = [(a, b) for a, b in plane if b % 2 == 0]
    mine_at = pl.ds(pl.multiple_of(rep * vis, vis), vis)

    def sel_copy(buf, send, recv, a, b):
        return remote(buf.at[0, mine_at], buf.at[a, mine_at], send.at[a, b], recv.at[a, b], peer(a, b))

    def weight_copy():
        return remote(wp_in.at[:, half_columns(1 - core)], swapped, w_send.at[0], w_recv.at[0], partner)

    def grad_copy():
        return remote(gradbuf.at[0], gradbuf.at[1], s_send.at[0], s_recv.at[0], partner)

    def p_copy(i, a, b):
        first = lax.rem(rep - b + replicas, replicas) * vis + lax.rem(sec + a, sections) * half
        return remote(
            psend.at[i, pl.ds(pl.multiple_of(first, half), half)],
            precv.at[i, a, b],
            p_send.at[i, a, b],
            p_recv.at[i, a, b],
            peer_back(a, b),
        )

    each(1, n, lambda o: k_copy(o).start())
    each(1, n, lambda o: v_copy(o).start())
    weight_copy().start()

    for c in small:
        c.wait()
    query_frames = frames[:, pl.ds(pl.multiple_of(me * tok, tok), tok)]
    row_at = lax.broadcasted_iota(jnp.int32, (tok, tok), 0)
    col_at = lax.broadcasted_iota(jnp.int32, (tok, tok), 1)
    hot_t = (lax.broadcasted_iota(jnp.int32, (tok, vis), 0) == rows[0]).astype(F32).astype(BF)
    eye = (row_at == col_at).astype(F32).astype(BF)
    hot = dot(hot_t, eye, (0, 0)).astype(BF)
    hots[0] = hot
    each(1, n, lambda o: h_copy(o).start())
    dots_row = jnp.concatenate([dots[h] for h in range(GROUP)], axis=1)

    def bias_for(o):
        first = lax.rem(me - o + n, n) * tok
        line = frames[:, pl.ds(pl.multiple_of(first, tok), tok)].astype(F32)
        key_frames = jnp.transpose(jnp.broadcast_to(line, (tok, tok)))
        allowed = (first + row_at <= me * tok + col_at) | (key_frames == query_frames.astype(F32))
        return jnp.where(allowed, 0.0, MASKED)

    def wide(bias):
        return jnp.concatenate([bias] * GROUP, axis=1)

    top[...] = jnp.full_like(top, MASKED)
    total[...] = jnp.zeros_like(total)
    gq_acc[...] = jnp.zeros_like(gq_acc)

    def first_pass(o, s, bias):
        s = s + wide(bias)
        sbuf[o] = s
        top[...] = jnp.maximum(top[...], jnp.max(s, axis=0, keepdims=True))

    def first_remote(o):
        k_copy(o).wait_recv()
        first_pass(o, dot(kbuf[o], qst[...]), bias_for(o))

    biases = [bias_for(o) for o in range(n if unrolled else 1)]
    loads[0].wait()
    for h, c in enumerate(q_loads):
        c.wait()
        at = pl.ds(h * HEAD, HEAD)
        qst[:, at] = jnp.transpose(qs[at, :])
    first_pass(0, dot(kbuf[0], qst[...]), biases[0])
    for h, c in enumerate(g_loads):
        c.wait()
        at = pl.ds(h * HEAD, HEAD)
        gst[:, at] = jnp.transpose(gs[at, :])
    if unrolled:
        for o in range(1, n):
            k_copy(o).wait_recv()
        s = dot(kbuf[1:n].reshape((n - 1) * tok, HEAD), qst[...])
        for o in range(1, n):
            first_pass(o, s[(o - 1) * tok : o * tok], biases[o])
    else:
        lax.fori_loop(1, n, lambda o, c: (first_remote(o), c)[1], 0)

    def second_pass(o):
        e = jnp.exp2((sbuf[o] - top[...]) * factor)
        sbuf[o] = e
        total[...] += jnp.sum(e, axis=0, keepdims=True)

    each(0, n, second_pass)
    total[...] = 1.0 / total[...]

    loads[1].wait()

    def third_pass(p, values):
        gp = dot(values, gst[...])
        gsc = (p * (gp - dots_row)).astype(BF)
        return gsc, dot(gsc, qs[...]) * scale, dot(p.astype(BF), gs[...])

    def send_rows(o, gk, gv):
        gk, gv = gk.astype(BF), gv.astype(BF)
        gsend[o, 0] = gk
        gsend[o, 1] = gv
        rsend[o] = dot(hots[o], jnp.concatenate([gk, gv], axis=1)).astype(BF)
        r_copy(o).start()

    def third_remote(o):
        v_copy(o).wait_recv()
        h_copy(o).wait_recv()
        gsc, gk, gv = third_pass(sbuf[o] * total[...], vbuf[o])
        gq_acc[...] += dot(kbuf[o], gsc, (0, 0))
        send_rows(o, gk, gv)

    if unrolled:
        for o in range(1, n):
            v_copy(o).wait_recv()
            h_copy(o).wait_recv()
        keys, values = kbuf[...].reshape(n * tok, HEAD), vbuf[...].reshape(n * tok, HEAD)
        gsc, gk_all, gv_all = third_pass(sbuf[...].reshape(n * tok, width) * total[...], values)
        for o in range(1, n):
            send_rows(o, gk_all[o * tok : (o + 1) * tok], gv_all[o * tok : (o + 1) * tok])
        gk, gv = gk_all[0:tok], gv_all[0:tok]
        gq_acc[...] = dot(keys, gsc, (0, 0))
    else:
        lax.fori_loop(1, n, lambda o, c: (third_remote(o), c)[1], 0)
        gsc, gk, gv = third_pass(sbuf[0] * total[...], vbuf[0])
        gq_acc[...] += dot(kbuf[0], gsc, (0, 0))

    gq = (gq_acc[...] * scale).astype(BF)
    for h in range(GROUP):
        gqsel[0, mine_at, h * HEAD : (h + 1) * HEAD] = dot(
            hot, gq[:, h * HEAD : (h + 1) * HEAD], (1, 1)
        ).astype(BF)
    for a, b in across:
        sel_copy(gqsel, a_send, a_recv, a, b).start()
    pass_copy(0, 0).start()
    each(1, n, lambda o: g_copy(o).start())

    def picked(x):
        return lax.dot_general(
            hot.astype(F32), x, (((1,), (0,)), ((), ())),
            precision=lax.Precision.HIGHEST, preferred_element_type=F32,
        )

    def gather(copy, read, start):
        def step(o, pair):
            copy(o).wait_recv()
            x, y = read(o)
            return pair[0] + x.astype(F32), pair[1] + y.astype(F32)

        if n <= 8:
            for o in range(1, n):
                start = step(o, start)
            return start
        return lax.fori_loop(1, n, step, start)

    rows_k, rows_v = gather(
        r_copy, lambda o: (rrecv[o, :, 0:HEAD], rrecv[o, :, HEAD : 2 * HEAD]), (picked(gk), picked(gv))
    )
    kvsel[0, mine_at, 0:HEAD] = rows_k.astype(BF)
    kvsel[0, mine_at, HEAD : 2 * HEAD] = rows_v.astype(BF)
    for a, b in plane:
        sel_copy(kvsel, b_send, b_recv, a, b).start()
    for a, b in across:
        sel_copy(gqsel, a_send, a_recv, a, b).wait_recv()
        pass_copy(a, b).start()

    loads[2].wait()
    loads[3].wait()
    part = width + 2 * HEAD
    for a, b in [(0, 0)] + across:
        pass_copy(a, b).wait_recv()

    def weight_rows(a, offset, size):
        first = lax.rem(sec - a + sections, sections) * part + offset
        return wq[:, pl.ds(pl.multiple_of(first, HEAD), size)]

    grad = dot(weight_rows(0, 0, width), gqsel[0], (1, 1))
    for a in range(1, sections):
        grad = grad + dot(weight_rows(a, 0, width), gqsel[a], (1, 1))
    for a, b in plane:
        sel_copy(kvsel, b_send, b_recv, a, b).wait_recv()
    for a in range(sections):
        grad = grad + dot(weight_rows(a, width, 2 * HEAD), kvsel[a], (1, 1))
    gradbuf[0] = grad.astype(BF)
    grad_copy().start()
    own = dot(gradbuf[0], wp[...], (0, 0))
    weight_copy().wait_recv()
    grad_copy().wait_recv()
    other = jnp.transpose(gradbuf[1])
    for i in range(CHUNKS):
        at = slice(i * columns, (i + 1) * columns)
        psend[i] = (own[:, at] + dot(other, swapped[:, at])).astype(BF)
        for a, b in plane:
            p_copy(i, a, b).start()

    gk, gv = gather(g_copy, lambda o: (grecv[o, 0], grecv[o, 1]), (gk, gv))
    dk_out[0] = gk.astype(BF)
    dv_out[0] = gv.astype(BF)

    slots = source.shape[2]
    at = lax.broadcasted_iota(jnp.int32, (slots, slots), 0)
    slot_of = lax.rem(at, half) * 4 + lax.div(at, half)
    moved_t = (slot_of == source[0]).astype(F32).astype(BF)

    near, far = [], []
    for i in range(CHUNKS):
        even = psend[i, pl.ds(pl.multiple_of(rep * vis + sec * half, half), half), :].astype(F32)
        odd = jnp.zeros_like(even)
        for a, b in plane:
            p_copy(i, a, b).wait_recv()
            if b % 2:
                odd = odd + precv[i, a, b].astype(F32)
            else:
                even = even + precv[i, a, b].astype(F32)
        near.append(even)
        far.append(odd)
    first = [jnp.where(core == 0, x, y) for x, y in zip(near, far)]
    second = [jnp.where(core == 0, y, x) for x, y in zip(near, far)]
    pieces = first + second
    merged = jnp.concatenate(pieces, axis=0).astype(BF)
    patch_out[0] = dot(moved_t, merged, (0, 0)).astype(BF)

    each(1, n, lambda o: k_copy(o).wait_send())
    each(1, n, lambda o: v_copy(o).wait_send())
    each(1, n, lambda o: g_copy(o).wait_send())
    each(1, n, lambda o: h_copy(o).wait_send())
    each(1, n, lambda o: r_copy(o).wait_send())
    pass_copy(0, 0).wait_send()
    for a, b in across:
        sel_copy(gqsel, a_send, a_recv, a, b).wait_send()
        pass_copy(a, b).wait_send()
    weight_copy().wait_send()
    grad_copy().wait_send()
    for a, b in plane:
        sel_copy(kvsel, b_send, b_recv, a, b).wait_send()
        for i in range(CHUNKS):
            p_copy(i, a, b).wait_send()


def hand_on(a, b, c, a_out, b_out, c_out):
    a_out[...] = a[...]
    b_out[...] = b[...]
    c_out[...] = c[...]


def solution(mesh):
    n, sections, replicas = mesh.shape["ctx"], mesh.shape["section"], mesh.shape["dp"]

    def shards(q, k, v, g, dots, frames, rows, source, wq, wp):
        tok, vis = k.shape[1], rows.shape[2]
        half = vis // 2
        width = GROUP * HEAD
        slots, quarter = source.shape[2], wp.shape[1] // 4
        anywhere = pl.BlockSpec(memory_space=pl.ANY)
        inside = pl.BlockSpec(memory_space=pltpu.VMEM)
        dma = pltpu.SemaphoreType.DMA
        model, side = wp.shape[0], wp.shape[1] // 2
        shapes = (
            jax.ShapeDtypeStruct(k.shape, BF),
            jax.ShapeDtypeStruct(v.shape, BF),
            jax.ShapeDtypeStruct((1, slots, quarter), BF),
        )
        outs = pl.pallas_call(
            functools.partial(kernel, n, sections, replicas),
            out_shape=shapes,
            in_specs=[anywhere] * 10,
            out_specs=(inside, inside, inside),
            scratch_shapes=[
                pltpu.VMEM((GROUP, 1, tok), F32),
                pltpu.VMEM(frames.shape, jnp.int32),
                pltpu.VMEM(rows.shape, jnp.int32),
                pltpu.VMEM(source.shape, jnp.int32),
                pltpu.VMEM((width, HEAD), BF),
                pltpu.VMEM((width, HEAD), BF),
                pltpu.VMEM((HEAD, width), BF),
                pltpu.VMEM((HEAD, width), BF),
                pltpu.VMEM((n, tok, HEAD), BF),
                pltpu.VMEM((n, tok, HEAD), BF),
                pltpu.VMEM((n, tok, width), F32),
                pltpu.VMEM((n, 2, tok, HEAD), BF),
                pltpu.VMEM((n, 2, tok, HEAD), BF),
                pltpu.VMEM((n, vis, tok), BF),
                pltpu.VMEM((n, vis, 2 * HEAD), BF),
                pltpu.VMEM((n, vis, 2 * HEAD), BF),
                pltpu.VMEM((model, wq.shape[0]), BF),
                pltpu.VMEM((model, side), BF),
                pltpu.VMEM((model, side), BF),
                pltpu.VMEM((1, width), F32),
                pltpu.VMEM((1, width), F32),
                pltpu.VMEM((HEAD, width), F32),
                pltpu.VMEM((sections, replicas * vis, width), BF),
                pltpu.VMEM((sections, replicas * vis, 2 * HEAD), BF),
                pltpu.VMEM((2, model, replicas * vis), BF),
                pltpu.VMEM((CHUNKS, replicas * vis, side // CHUNKS), BF),
                pltpu.VMEM((CHUNKS, sections, replicas, half, side // CHUNKS), BF),
                dma((8 + 2 * GROUP,)),
                dma((n,)), dma((n,)), dma((n,)), dma((n,)), dma((n,)), dma((n,)),
                dma((sections, replicas)), dma((sections, replicas)),
                dma((sections, replicas)), dma((sections, replicas)),
                dma((CHUNKS, sections, replicas)), dma((CHUNKS, sections, replicas)),
                dma((1,)), dma((1,)), dma((1,)), dma((1,)),
                dma((n,)), dma((n,)), dma((n,)), dma((n,)),
            ],
            compiler_params=pltpu.CompilerParams(
                collective_id=0, has_side_effects=True, vmem_limit_bytes=56 * 1024 * 1024
            ),
        )(q, k, v, g, dots.transpose(1, 0, 2), frames, rows, source, wq.T, wp)
        return pl.pallas_call(
            hand_on,
            out_shape=shapes,
            in_specs=[inside] * 3,
            out_specs=(inside,) * 3,
        )(*outs)

    placed = (
        P("dp", "ctx", "section"),
        P("dp", "ctx", "section"),
        P("dp", "ctx", "section"),
        P("dp", "ctx", "section"),
        P("dp", "section", "ctx"),
        P("dp", None),
        P("dp", "ctx", None),
        P("dp", ("ctx", "section"), None),
        P(None, ("section", "dp")),
        P(("section", "dp"), None),
    )
    return jax.shard_map(
        shards,
        mesh=mesh,
        in_specs=placed,
        out_specs=(
            P("dp", "ctx", "section"),
            P("dp", "ctx", "section"),
            P("dp", ("ctx", "section"), None),
        ),
        check_vma=False,
    )
```

```python
import functools
import math

import jax
import jax.numpy as jnp
from jax import lax
from jax.experimental import pallas as pl
from jax.experimental.pallas import tpu as pltpu
from jax.sharding import PartitionSpec as P

HEAD = 128
GROUP = 7
MASKED = -1e30
MESH = pl.DeviceIdType.MESH
CHUNKS = 4
BF = jnp.bfloat16
F32 = jnp.float32


def dot(a, b, over=(1, 0)):
    return lax.dot_general(a, b, (((over[0],), (over[1],)), ((), ())), preferred_element_type=F32)


def kernel(
    n, sections, replicas,
    q_in, k_in, v_in, g_in, dots_in, frames_in, rows_in, source_in, wq_in, wp_in,
    dk_out, dv_out, patch_out,
    dots, frames, rows, source, qs, gs, qst, gst, kbuf, vbuf, sbuf, gsend, grecv, hots, rsend, rrecv, wq, wp, top, total, gq_acc, gqsel, kvsel, psend, precv,
    load_sem, k_send, k_recv, v_send, v_recv, g_send, g_recv, a_send, a_recv, b_send, b_recv, p_send, p_recv, h_send, h_recv, r_send, r_recv,
):
    me = lax.axis_index("ctx")
    sec = lax.axis_index("section")
    rep = lax.axis_index("dp")
    tok = k_in.shape[1]
    vis = rows.shape[2]
    unrolled = n <= 8
    half = vis // 2
    width = GROUP * HEAD
    scale = 1.0 / math.sqrt(HEAD)
    factor = scale * math.log2(math.e)
    plane = [(a, b) for a in range(sections) for b in range(replicas) if a or b]

    def each(low, high, body):
        if n <= 8:
            for at in range(low, high):
                body(at)
        else:
            lax.fori_loop(low, high, lambda at, c: (body(at), c)[1], 0)

    def ahead(o):
        return {"ctx": lax.rem(me + o, n)}

    def behind(o):
        return {"ctx": lax.rem(me - o + n, n)}

    def peer(a, b):
        return {"section": lax.rem(sec + a, sections), "dp": lax.rem(rep + b, replicas)}

    def peer_back(a, b):
        return {"section": lax.rem(sec + a, sections), "dp": lax.rem(rep - b + replicas, replicas)}

    core = lax.rem(rep, 2)
    partner = {"dp": rep + 1 - 2 * core}
    columns = wp.shape[1] // CHUNKS

    barrier = pltpu.get_barrier_semaphore()
    each(1, n, lambda o: pl.semaphore_signal(barrier, inc=1, device_id=ahead(o), device_id_type=MESH))
    for a, b in plane:
        pl.semaphore_signal(barrier, inc=1, device_id=peer(a, b), device_id_type=MESH)

    loads = [
        pltpu.make_async_copy(k_in.at[0], kbuf.at[0], load_sem.at[0]),
        pltpu.make_async_copy(v_in.at[0], vbuf.at[0], load_sem.at[1]),
        pltpu.make_async_copy(wq_in, wq, load_sem.at[2]),
        pltpu.make_async_copy(wp_in, wp, load_sem.at[3]),
    ]
    q_loads = [
        pltpu.make_async_copy(
            q_in.at[0, :, pl.ds(h * HEAD, HEAD)], qs.at[pl.ds(h * HEAD, HEAD), :], load_sem.at[4 + h]
        )
        for h in range(GROUP)
    ]
    g_loads = [
        pltpu.make_async_copy(
            g_in.at[0, :, pl.ds(h * HEAD, HEAD)], gs.at[pl.ds(h * HEAD, HEAD), :], load_sem.at[4 + GROUP + h]
        )
        for h in range(GROUP)
    ]
    small = [
        pltpu.make_async_copy(x, y, load_sem.at[4 + 2 * GROUP + i])
        for i, (x, y) in enumerate(((frames_in, frames), (rows_in, rows), (dots_in, dots), (source_in, source)))
    ]
    loads[0].start()
    for c in small:
        c.start()
    for c in q_loads:
        c.start()
    loads[1].start()
    for c in g_loads:
        c.start()
    loads[2].start()
    loads[3].start()
    pl.semaphore_wait(barrier, (n - 1) + len(plane))

    def remote(src, dst, send, recv, device):
        return pltpu.make_async_remote_copy(
            src_ref=src, dst_ref=dst, send_sem=send, recv_sem=recv, device_id=device, device_id_type=MESH
        )

    def k_copy(o):
        return remote(k_in.at[0], kbuf.at[o], k_send.at[o], k_recv.at[o], ahead(o))

    def v_copy(o):
        return remote(v_in.at[0], vbuf.at[o], v_send.at[o], v_recv.at[o], ahead(o))

    def g_copy(o):
        return remote(gsend.at[o], grecv.at[o], g_send.at[o], g_recv.at[o], behind(o))

    def h_copy(o):
        return remote(hots.at[0], hots.at[o], h_send.at[o], h_recv.at[o], ahead(o))

    def r_copy(o):
        return remote(rsend.at[o], rrecv.at[o], r_send.at[o], r_recv.at[o], behind(o))

    def pass_copy(a, b):
        at = pl.ds(pl.multiple_of(lax.rem(rep - b + replicas, replicas) * vis, vis), vis)
        return remote(gqsel.at[a, at], gqsel.at[a, at], a_send.at[a, b + 1], a_recv.at[a, b + 1], partner)

    across = [(a, b) for a, b in plane if b % 2 == 0]
    mine_at = pl.ds(pl.multiple_of(rep * vis, vis), vis)

    def sel_copy(buf, send, recv, a, b):
        return remote(buf.at[0, mine_at], buf.at[a, mine_at], send.at[a, b], recv.at[a, b], peer(a, b))

    def p_copy(i, a, b):
        first = lax.rem(rep - b + replicas, replicas) * vis + lax.rem(sec + a, sections) * half
        return remote(
            psend.at[i, pl.ds(pl.multiple_of(first, half), half)],
            precv.at[i, a, b],
            p_send.at[i, a, b],
            p_recv.at[i, a, b],
            peer_back(a, b),
        )

    each(1, n, lambda o: k_copy(o).start())
    each(1, n, lambda o: v_copy(o).start())

    for c in small:
        c.wait()
    query_frames = frames[:, pl.ds(pl.multiple_of(me * tok, tok), tok)]
    row_at = lax.broadcasted_iota(jnp.int32, (tok, tok), 0)
    col_at = lax.broadcasted_iota(jnp.int32, (tok, tok), 1)
    hot_t = (lax.broadcasted_iota(jnp.int32, (tok, vis), 0) == rows[0]).astype(F32).astype(BF)
    eye = (row_at == col_at).astype(F32).astype(BF)
    hot = dot(hot_t, eye, (0, 0)).astype(BF)
    hots[0] = hot
    each(1, n, lambda o: h_copy(o).start())
    dots_row = jnp.concatenate([dots[h] for h in range(GROUP)], axis=1)

    def bias_for(o):
        first = lax.rem(me - o + n, n) * tok
        line = frames[:, pl.ds(pl.multiple_of(first, tok), tok)].astype(F32)
        key_frames = jnp.transpose(jnp.broadcast_to(line, (tok, tok)))
        allowed = (first + row_at <= me * tok + col_at) | (key_frames == query_frames.astype(F32))
        return jnp.where(allowed, 0.0, MASKED)

    def wide(bias):
        return jnp.concatenate([bias] * GROUP, axis=1)

    top[...] = jnp.full_like(top, MASKED)
    total[...] = jnp.zeros_like(total)
    gq_acc[...] = jnp.zeros_like(gq_acc)

    def first_pass(o, s, bias):
        s = s + wide(bias)
        sbuf[o] = s
        top[...] = jnp.maximum(top[...], jnp.max(s, axis=0, keepdims=True))

    def first_remote(o):
        k_copy(o).wait_recv()
        first_pass(o, dot(kbuf[o], qst[...]), bias_for(o))

    biases = [bias_for(o) for o in range(n if unrolled else 1)]
    loads[0].wait()
    for h, c in enumerate(q_loads):
        c.wait()
        at = pl.ds(h * HEAD, HEAD)
        qst[:, at] = jnp.transpose(qs[at, :])
    first_pass(0, dot(kbuf[0], qst[...]), biases[0])
    for h, c in enumerate(g_loads):
        c.wait()
        at = pl.ds(h * HEAD, HEAD)
        gst[:, at] = jnp.transpose(gs[at, :])
    if unrolled:
        for o in range(1, n):
            k_copy(o).wait_recv()
        s = dot(kbuf[1:n].reshape((n - 1) * tok, HEAD), qst[...])
        for o in range(1, n):
            first_pass(o, s[(o - 1) * tok : o * tok], biases[o])
    else:
        lax.fori_loop(1, n, lambda o, c: (first_remote(o), c)[1], 0)

    def second_pass(o):
        e = jnp.exp2((sbuf[o] - top[...]) * factor)
        sbuf[o] = e
        total[...] += jnp.sum(e, axis=0, keepdims=True)

    each(0, n, second_pass)
    total[...] = 1.0 / total[...]

    loads[1].wait()

    def third_pass(p, values):
        gp = dot(values, gst[...])
        gsc = (p * (gp - dots_row)).astype(BF)
        return gsc, dot(gsc, qs[...]) * scale, dot(p.astype(BF), gs[...])

    def send_rows(o, gk, gv):
        gk, gv = gk.astype(BF), gv.astype(BF)
        gsend[o, 0] = gk
        gsend[o, 1] = gv
        rsend[o] = dot(hots[o], jnp.concatenate([gk, gv], axis=1)).astype(BF)
        r_copy(o).start()

    def third_remote(o):
        v_copy(o).wait_recv()
        h_copy(o).wait_recv()
        gsc, gk, gv = third_pass(sbuf[o] * total[...], vbuf[o])
        gq_acc[...] += dot(kbuf[o], gsc, (0, 0))
        send_rows(o, gk, gv)

    if unrolled:
        for o in range(1, n):
            v_copy(o).wait_recv()
            h_copy(o).wait_recv()
        keys, values = kbuf[...].reshape(n * tok, HEAD), vbuf[...].reshape(n * tok, HEAD)
        gsc, gk_all, gv_all = third_pass(sbuf[...].reshape(n * tok, width) * total[...], values)
        for o in range(1, n):
            send_rows(o, gk_all[o * tok : (o + 1) * tok], gv_all[o * tok : (o + 1) * tok])
        gk, gv = gk_all[0:tok], gv_all[0:tok]
        gq_acc[...] = dot(keys, gsc, (0, 0))
    else:
        lax.fori_loop(1, n, lambda o, c: (third_remote(o), c)[1], 0)
        gsc, gk, gv = third_pass(sbuf[0] * total[...], vbuf[0])
        gq_acc[...] += dot(kbuf[0], gsc, (0, 0))

    gq = (gq_acc[...] * scale).astype(BF)
    for h in range(GROUP):
        gqsel[0, mine_at, h * HEAD : (h + 1) * HEAD] = dot(
            hot, gq[:, h * HEAD : (h + 1) * HEAD], (1, 1)
        ).astype(BF)
    for a, b in across:
        sel_copy(gqsel, a_send, a_recv, a, b).start()
    pass_copy(0, 0).start()
    each(1, n, lambda o: g_copy(o).start())

    def picked(x):
        return lax.dot_general(
            hot.astype(F32), x, (((1,), (0,)), ((), ())),
            precision=lax.Precision.HIGHEST, preferred_element_type=F32,
        )

    def gather(copy, read, start):
        def step(o, pair):
            copy(o).wait_recv()
            x, y = read(o)
            return pair[0] + x.astype(F32), pair[1] + y.astype(F32)

        if n <= 8:
            for o in range(1, n):
                start = step(o, start)
            return start
        return lax.fori_loop(1, n, step, start)

    rows_k, rows_v = gather(
        r_copy, lambda o: (rrecv[o, :, 0:HEAD], rrecv[o, :, HEAD : 2 * HEAD]), (picked(gk), picked(gv))
    )
    kvsel[0, mine_at, 0:HEAD] = rows_k.astype(BF)
    kvsel[0, mine_at, HEAD : 2 * HEAD] = rows_v.astype(BF)
    for a, b in plane:
        sel_copy(kvsel, b_send, b_recv, a, b).start()
    for a, b in across:
        sel_copy(gqsel, a_send, a_recv, a, b).wait_recv()
        pass_copy(a, b).start()

    loads[2].wait()
    loads[3].wait()
    part = width + 2 * HEAD
    for a, b in [(0, 0)] + across:
        pass_copy(a, b).wait_recv()

    def weight_rows(a, offset, size):
        first = lax.rem(sec - a + sections, sections) * part + offset
        return wq[:, pl.ds(pl.multiple_of(first, HEAD), size)]

    grad = dot(weight_rows(0, 0, width), gqsel[0], (1, 1))
    for a in range(1, sections):
        grad = grad + dot(weight_rows(a, 0, width), gqsel[a], (1, 1))
    for a, b in plane:
        sel_copy(kvsel, b_send, b_recv, a, b).wait_recv()
    for a in range(sections):
        grad = grad + dot(weight_rows(a, width, 2 * HEAD), kvsel[a], (1, 1))
    grad = jnp.transpose(grad.astype(BF))
    for i in range(CHUNKS):
        at = slice(i * columns, (i + 1) * columns)
        psend[i] = dot(grad, wp[:, at]).astype(BF)
        for a, b in plane:
            p_copy(i, a, b).start()

    gk, gv = gather(g_copy, lambda o: (grecv[o, 0], grecv[o, 1]), (gk, gv))
    dk_out[0] = gk.astype(BF)
    dv_out[0] = gv.astype(BF)

    slots = source.shape[2]
    at = lax.broadcasted_iota(jnp.int32, (slots, slots), 0)
    slot_of = lax.rem(at, half) * 4 + lax.div(at, half)
    moved_t = (slot_of == source[0]).astype(F32).astype(BF)

    pieces = []
    for i in range(CHUNKS):
        mine = psend[i, pl.ds(pl.multiple_of(rep * vis + sec * half, half), half), :].astype(F32)
        for a, b in plane:
            p_copy(i, a, b).wait_recv()
            mine = mine + precv[i, a, b].astype(F32)
        pieces.append(mine)
    merged = jnp.concatenate(pieces, axis=0).astype(BF)
    patch_out[0] = dot(moved_t, merged, (0, 0)).astype(BF)

    each(1, n, lambda o: k_copy(o).wait_send())
    each(1, n, lambda o: v_copy(o).wait_send())
    each(1, n, lambda o: g_copy(o).wait_send())
    each(1, n, lambda o: h_copy(o).wait_send())
    each(1, n, lambda o: r_copy(o).wait_send())
    pass_copy(0, 0).wait_send()
    for a, b in across:
        sel_copy(gqsel, a_send, a_recv, a, b).wait_send()
        pass_copy(a, b).wait_send()
    for a, b in plane:
        sel_copy(kvsel, b_send, b_recv, a, b).wait_send()
        for i in range(CHUNKS):
            p_copy(i, a, b).wait_send()


def hand_on(a, b, c, a_out, b_out, c_out):
    a_out[...] = a[...]
    b_out[...] = b[...]
    c_out[...] = c[...]


def solution(mesh):
    n, sections, replicas = mesh.shape["ctx"], mesh.shape["section"], mesh.shape["dp"]

    def shards(q, k, v, g, dots, frames, rows, source, wq, wp):
        tok, vis = k.shape[1], rows.shape[2]
        half = vis // 2
        width = GROUP * HEAD
        slots, quarter = source.shape[2], wp.shape[1] // 4
        anywhere = pl.BlockSpec(memory_space=pl.ANY)
        inside = pl.BlockSpec(memory_space=pltpu.VMEM)
        dma = pltpu.SemaphoreType.DMA
        model, side = wp.shape[0], wp.shape[1]
        shapes = (
            jax.ShapeDtypeStruct(k.shape, BF),
            jax.ShapeDtypeStruct(v.shape, BF),
            jax.ShapeDtypeStruct((1, slots, quarter), BF),
        )
        outs = pl.pallas_call(
            functools.partial(kernel, n, sections, replicas),
            out_shape=shapes,
            in_specs=[anywhere] * 10,
            out_specs=(inside, inside, inside),
            scratch_shapes=[
                pltpu.VMEM((GROUP, 1, tok), F32),
                pltpu.VMEM(frames.shape, jnp.int32),
                pltpu.VMEM(rows.shape, jnp.int32),
                pltpu.VMEM(source.shape, jnp.int32),
                pltpu.VMEM((width, HEAD), BF),
                pltpu.VMEM((width, HEAD), BF),
                pltpu.VMEM((HEAD, width), BF),
                pltpu.VMEM((HEAD, width), BF),
                pltpu.VMEM((n, tok, HEAD), BF),
                pltpu.VMEM((n, tok, HEAD), BF),
                pltpu.VMEM((n, tok, width), F32),
                pltpu.VMEM((n, 2, tok, HEAD), BF),
                pltpu.VMEM((n, 2, tok, HEAD), BF),
                pltpu.VMEM((n, vis, tok), BF),
                pltpu.VMEM((n, vis, 2 * HEAD), BF),
                pltpu.VMEM((n, vis, 2 * HEAD), BF),
                pltpu.VMEM((model, wq.shape[0]), BF),
                pltpu.VMEM((model, side), BF),
                pltpu.VMEM((1, width), F32),
                pltpu.VMEM((1, width), F32),
                pltpu.VMEM((HEAD, width), F32),
                pltpu.VMEM((sections, replicas * vis, width), BF),
                pltpu.VMEM((sections, replicas * vis, 2 * HEAD), BF),
                pltpu.VMEM((CHUNKS, replicas * vis, side // CHUNKS), BF),
                pltpu.VMEM((CHUNKS, sections, replicas, half, side // CHUNKS), BF),
                dma((8 + 2 * GROUP,)),
                dma((n,)), dma((n,)), dma((n,)), dma((n,)), dma((n,)), dma((n,)),
                dma((sections, replicas)), dma((sections, replicas)),
                dma((sections, replicas)), dma((sections, replicas)),
                dma((CHUNKS, sections, replicas)), dma((CHUNKS, sections, replicas)),
                dma((n,)), dma((n,)), dma((n,)), dma((n,)),
            ],
            compiler_params=pltpu.CompilerParams(
                collective_id=0, has_side_effects=True, vmem_limit_bytes=56 * 1024 * 1024
            ),
        )(q, k, v, g, dots.transpose(1, 0, 2), frames, rows, source, wq.T, wp)
        return pl.pallas_call(
            hand_on,
            out_shape=shapes,
            in_specs=[inside] * 3,
            out_specs=(inside,) * 3,
        )(*outs)

    placed = (
        P("dp", "ctx", "section"),
        P("dp", "ctx", "section"),
        P("dp", "ctx", "section"),
        P("dp", "ctx", "section"),
        P("dp", "section", "ctx"),
        P("dp", None),
        P("dp", "ctx", None),
        P("dp", ("ctx", "section"), None),
        P(None, ("section", "dp")),
        P(("section", "dp"), None),
    )
    return jax.shard_map(
        shards,
        mesh=mesh,
        in_specs=placed,
        out_specs=(
            P("dp", "ctx", "section"),
            P("dp", "ctx", "section"),
            P("dp", ("ctx", "section"), None),
        ),
        check_vma=False,
    )
```

```python
import functools
import math

import jax
import jax.numpy as jnp
from jax import lax
from jax.experimental import pallas as pl
from jax.experimental.pallas import tpu as pltpu
from jax.sharding import PartitionSpec as P

HEAD = 128
GROUP = 7
MASKED = -1e30
MESH = pl.DeviceIdType.MESH
CHUNKS = 2
BF = jnp.bfloat16
F32 = jnp.float32


def dot(a, b, over=(1, 0)):
    return lax.dot_general(a, b, (((over[0],), (over[1],)), ((), ())), preferred_element_type=F32)


def kernel(
    n, sections, replicas,
    q_in, k_in, v_in, g_in, dots_in, frames_in, rows_in, source_in, wq_in, wp_in,
    dk_out, dv_out, patch_out,
    dots, frames, rows, source, qs, gs, qst, gst, kbuf, vbuf, sbuf, gsend, grecv, hots, rsend, rrecv, wq, wp, swapped, top, total, gq_acc, gqsel, kvsel, gradbuf, psend, precv,
    load_sem, k_send, k_recv, v_send, v_recv, g_send, g_recv, a_send, a_recv, b_send, b_recv, p_send, p_recv, w_send, w_recv, s_send, s_recv, h_send, h_recv, r_send, r_recv,
):
    me = lax.axis_index("ctx")
    sec = lax.axis_index("section")
    rep = lax.axis_index("dp")
    tok = k_in.shape[1]
    vis = rows.shape[2]
    unrolled = n <= 8
    half = vis // 2
    width = GROUP * HEAD
    scale = 1.0 / math.sqrt(HEAD)
    factor = scale * math.log2(math.e)
    plane = [(a, b) for a in range(sections) for b in range(replicas) if a or b]

    def each(low, high, body):
        if n <= 8:
            for at in range(low, high):
                body(at)
        else:
            lax.fori_loop(low, high, lambda at, c: (body(at), c)[1], 0)

    def ahead(o):
        return {"ctx": lax.rem(me + o, n)}

    def behind(o):
        return {"ctx": lax.rem(me - o + n, n)}

    def peer(a, b):
        return {"section": lax.rem(sec + a, sections), "dp": lax.rem(rep + b, replicas)}

    def peer_back(a, b):
        return {"section": lax.rem(sec + a, sections), "dp": lax.rem(rep - b + replicas, replicas)}

    core = lax.rem(rep, 2)
    partner = {"dp": rep + 1 - 2 * core}
    columns = wp.shape[1] // CHUNKS

    def half_columns(which):
        return pl.ds(pl.multiple_of(which * wp.shape[1], wp.shape[1]), wp.shape[1])

    barrier = pltpu.get_barrier_semaphore()
    each(1, n, lambda o: pl.semaphore_signal(barrier, inc=1, device_id=ahead(o), device_id_type=MESH))
    for a, b in plane:
        pl.semaphore_signal(barrier, inc=1, device_id=peer(a, b), device_id_type=MESH)

    loads = [
        pltpu.make_async_copy(k_in.at[0], kbuf.at[0], load_sem.at[0]),
        pltpu.make_async_copy(v_in.at[0], vbuf.at[0], load_sem.at[1]),
        pltpu.make_async_copy(wq_in, wq, load_sem.at[2]),
        pltpu.make_async_copy(wp_in.at[:, half_columns(core)], wp, load_sem.at[3]),
    ]
    q_loads = [
        pltpu.make_async_copy(
            q_in.at[0, :, pl.ds(h * HEAD, HEAD)], qs.at[pl.ds(h * HEAD, HEAD), :], load_sem.at[4 + h]
        )
        for h in range(GROUP)
    ]
    g_loads = [
        pltpu.make_async_copy(
            g_in.at[0, :, pl.ds(h * HEAD, HEAD)], gs.at[pl.ds(h * HEAD, HEAD), :], load_sem.at[4 + GROUP + h]
        )
        for h in range(GROUP)
    ]
    small = [
        pltpu.make_async_copy(x, y, load_sem.at[4 + 2 * GROUP + i])
        for i, (x, y) in enumerate(((frames_in, frames), (rows_in, rows), (dots_in, dots), (source_in, source)))
    ]
    loads[0].start()
    for c in small:
        c.start()
    for c in q_loads:
        c.start()
    loads[1].start()
    for c in g_loads:
        c.start()
    loads[2].start()
    loads[3].start()
    pl.semaphore_wait(barrier, (n - 1) + len(plane))

    def remote(src, dst, send, recv, device):
        return pltpu.make_async_remote_copy(
            src_ref=src, dst_ref=dst, send_sem=send, recv_sem=recv, device_id=device, device_id_type=MESH
        )

    def k_copy(o):
        return remote(k_in.at[0], kbuf.at[o], k_send.at[o], k_recv.at[o], ahead(o))

    def v_copy(o):
        return remote(v_in.at[0], vbuf.at[o], v_send.at[o], v_recv.at[o], ahead(o))

    def g_copy(o):
        return remote(gsend.at[o], grecv.at[o], g_send.at[o], g_recv.at[o], behind(o))

    def h_copy(o):
        return remote(hots.at[0], hots.at[o], h_send.at[o], h_recv.at[o], ahead(o))

    def r_copy(o):
        return remote(rsend.at[o], rrecv.at[o], r_send.at[o], r_recv.at[o], behind(o))

    mine_at = pl.ds(pl.multiple_of(rep * vis, vis), vis)

    def sel_copy(buf, send, recv, a, b):
        return remote(buf.at[0, mine_at], buf.at[a, mine_at], send.at[a, b], recv.at[a, b], peer(a, b))

    def weight_copy():
        return remote(wp_in.at[:, half_columns(1 - core)], swapped, w_send.at[0], w_recv.at[0], partner)

    def grad_copy():
        return remote(gradbuf.at[0], gradbuf.at[1], s_send.at[0], s_recv.at[0], partner)

    def p_copy(i, a, b):
        first = lax.rem(rep - b + replicas, replicas) * vis + lax.rem(sec + a, sections) * half
        return remote(
            psend.at[i, pl.ds(pl.multiple_of(first, half), half)],
            precv.at[i, a, b],
            p_send.at[i, a, b],
            p_recv.at[i, a, b],
            peer_back(a, b),
        )

    each(1, n, lambda o: k_copy(o).start())
    each(1, n, lambda o: v_copy(o).start())
    weight_copy().start()

    for c in small:
        c.wait()
    query_frames = frames[:, pl.ds(pl.multiple_of(me * tok, tok), tok)]
    row_at = lax.broadcasted_iota(jnp.int32, (tok, tok), 0)
    col_at = lax.broadcasted_iota(jnp.int32, (tok, tok), 1)
    hot_t = (lax.broadcasted_iota(jnp.int32, (tok, vis), 0) == rows[0]).astype(F32).astype(BF)
    eye = (row_at == col_at).astype(F32).astype(BF)
    hot = dot(hot_t, eye, (0, 0)).astype(BF)
    hots[0] = hot
    each(1, n, lambda o: h_copy(o).start())
    dots_row = jnp.concatenate([dots[h] for h in range(GROUP)], axis=1)

    def bias_for(o):
        first = lax.rem(me - o + n, n) * tok
        line = frames[:, pl.ds(pl.multiple_of(first, tok), tok)].astype(F32)
        key_frames = jnp.transpose(jnp.broadcast_to(line, (tok, tok)))
        allowed = (first + row_at <= me * tok + col_at) | (key_frames == query_frames.astype(F32))
        return jnp.where(allowed, 0.0, MASKED)

    def wide(bias):
        return jnp.concatenate([bias] * GROUP, axis=1)

    top[...] = jnp.full_like(top, MASKED)
    total[...] = jnp.zeros_like(total)
    gq_acc[...] = jnp.zeros_like(gq_acc)

    def first_pass(o, s, bias):
        s = s + wide(bias)
        sbuf[o] = s
        top[...] = jnp.maximum(top[...], jnp.max(s, axis=0, keepdims=True))

    def first_remote(o):
        k_copy(o).wait_recv()
        first_pass(o, dot(kbuf[o], qst[...]), bias_for(o))

    biases = [bias_for(o) for o in range(n if unrolled else 1)]
    loads[0].wait()
    for h, c in enumerate(q_loads):
        c.wait()
        at = pl.ds(h * HEAD, HEAD)
        qst[:, at] = jnp.transpose(qs[at, :])
    first_pass(0, dot(kbuf[0], qst[...]), biases[0])
    for h, c in enumerate(g_loads):
        c.wait()
        at = pl.ds(h * HEAD, HEAD)
        gst[:, at] = jnp.transpose(gs[at, :])
    if unrolled:
        for o in range(1, n):
            k_copy(o).wait_recv()
        s = dot(kbuf[1:n].reshape((n - 1) * tok, HEAD), qst[...])
        for o in range(1, n):
            first_pass(o, s[(o - 1) * tok : o * tok], biases[o])
    else:
        lax.fori_loop(1, n, lambda o, c: (first_remote(o), c)[1], 0)

    def second_pass(o):
        e = jnp.exp2((sbuf[o] - top[...]) * factor)
        sbuf[o] = e
        total[...] += jnp.sum(e, axis=0, keepdims=True)

    each(0, n, second_pass)
    total[...] = 1.0 / total[...]

    loads[1].wait()

    def third_pass(p, values):
        gp = dot(values, gst[...])
        gsc = (p * (gp - dots_row)).astype(BF)
        return gsc, dot(gsc, qs[...]) * scale, dot(p.astype(BF), gs[...])

    def send_rows(o, gk, gv):
        gk, gv = gk.astype(BF), gv.astype(BF)
        gsend[o, 0] = gk
        gsend[o, 1] = gv
        rsend[o] = dot(hots[o], jnp.concatenate([gk, gv], axis=1)).astype(BF)
        r_copy(o).start()

    def third_remote(o):
        v_copy(o).wait_recv()
        h_copy(o).wait_recv()
        gsc, gk, gv = third_pass(sbuf[o] * total[...], vbuf[o])
        gq_acc[...] += dot(kbuf[o], gsc, (0, 0))
        send_rows(o, gk, gv)

    if unrolled:
        for o in range(1, n):
            v_copy(o).wait_recv()
            h_copy(o).wait_recv()
        keys, values = kbuf[...].reshape(n * tok, HEAD), vbuf[...].reshape(n * tok, HEAD)
        gsc, gk_all, gv_all = third_pass(sbuf[...].reshape(n * tok, width) * total[...], values)
        for o in range(1, n):
            send_rows(o, gk_all[o * tok : (o + 1) * tok], gv_all[o * tok : (o + 1) * tok])
        gk, gv = gk_all[0:tok], gv_all[0:tok]
        gq_acc[...] = dot(keys, gsc, (0, 0))
    else:
        lax.fori_loop(1, n, lambda o, c: (third_remote(o), c)[1], 0)
        gsc, gk, gv = third_pass(sbuf[0] * total[...], vbuf[0])
        gq_acc[...] += dot(kbuf[0], gsc, (0, 0))

    gq = (gq_acc[...] * scale).astype(BF)
    for h in range(GROUP):
        gqsel[0, mine_at, h * HEAD : (h + 1) * HEAD] = dot(
            hot, gq[:, h * HEAD : (h + 1) * HEAD], (1, 1)
        ).astype(BF)
    for a, b in plane:
        sel_copy(gqsel, a_send, a_recv, a, b).start()
    each(1, n, lambda o: g_copy(o).start())

    def picked(x):
        return lax.dot_general(
            hot.astype(F32), x, (((1,), (0,)), ((), ())),
            precision=lax.Precision.HIGHEST, preferred_element_type=F32,
        )

    def gather(copy, read, start):
        def step(o, pair):
            copy(o).wait_recv()
            x, y = read(o)
            return pair[0] + x.astype(F32), pair[1] + y.astype(F32)

        if n <= 8:
            for o in range(1, n):
                start = step(o, start)
            return start
        return lax.fori_loop(1, n, step, start)

    rows_k, rows_v = gather(
        r_copy, lambda o: (rrecv[o, :, 0:HEAD], rrecv[o, :, HEAD : 2 * HEAD]), (picked(gk), picked(gv))
    )
    kvsel[0, mine_at, 0:HEAD] = rows_k.astype(BF)
    kvsel[0, mine_at, HEAD : 2 * HEAD] = rows_v.astype(BF)
    for a, b in plane:
        sel_copy(kvsel, b_send, b_recv, a, b).start()

    loads[2].wait()
    loads[3].wait()
    part = width + 2 * HEAD
    for a, b in plane:
        sel_copy(gqsel, a_send, a_recv, a, b).wait_recv()

    def weight_rows(a, offset, size):
        first = lax.rem(sec - a + sections, sections) * part + offset
        return wq[:, pl.ds(pl.multiple_of(first, HEAD), size)]

    grad = dot(weight_rows(0, 0, width), gqsel[0], (1, 1))
    for a in range(1, sections):
        grad = grad + dot(weight_rows(a, 0, width), gqsel[a], (1, 1))
    for a, b in plane:
        sel_copy(kvsel, b_send, b_recv, a, b).wait_recv()
    for a in range(sections):
        grad = grad + dot(weight_rows(a, width, 2 * HEAD), kvsel[a], (1, 1))
    gradbuf[0] = grad.astype(BF)
    grad_copy().start()
    own = dot(gradbuf[0], wp[...], (0, 0))
    weight_copy().wait_recv()
    grad_copy().wait_recv()
    other = jnp.transpose(gradbuf[1])
    for i in range(CHUNKS):
        at = slice(i * columns, (i + 1) * columns)
        psend[i] = (own[:, at] + dot(other, swapped[:, at])).astype(BF)
        for a, b in plane:
            p_copy(i, a, b).start()

    gk, gv = gather(g_copy, lambda o: (grecv[o, 0], grecv[o, 1]), (gk, gv))
    dk_out[0] = gk.astype(BF)
    dv_out[0] = gv.astype(BF)

    slots = source.shape[2]
    at = lax.broadcasted_iota(jnp.int32, (slots, slots), 0)
    slot_of = lax.rem(at, half) * 4 + lax.div(at, half)
    moved_t = (slot_of == source[0]).astype(F32).astype(BF)

    near, far = [], []
    for i in range(CHUNKS):
        even = psend[i, pl.ds(pl.multiple_of(rep * vis + sec * half, half), half), :].astype(F32)
        odd = jnp.zeros_like(even)
        for a, b in plane:
            p_copy(i, a, b).wait_recv()
            if b % 2:
                odd = odd + precv[i, a, b].astype(F32)
            else:
                even = even + precv[i, a, b].astype(F32)
        near.append(even)
        far.append(odd)
    first = [jnp.where(core == 0, x, y) for x, y in zip(near, far)]
    second = [jnp.where(core == 0, y, x) for x, y in zip(near, far)]
    pieces = first + second
    merged = jnp.concatenate(pieces, axis=0).astype(BF)
    patch_out[0] = dot(moved_t, merged, (0, 0)).astype(BF)

    each(1, n, lambda o: k_copy(o).wait_send())
    each(1, n, lambda o: v_copy(o).wait_send())
    each(1, n, lambda o: g_copy(o).wait_send())
    each(1, n, lambda o: h_copy(o).wait_send())
    each(1, n, lambda o: r_copy(o).wait_send())
    for a, b in plane:
        sel_copy(gqsel, a_send, a_recv, a, b).wait_send()
    weight_copy().wait_send()
    grad_copy().wait_send()
    for a, b in plane:
        sel_copy(kvsel, b_send, b_recv, a, b).wait_send()
        for i in range(CHUNKS):
            p_copy(i, a, b).wait_send()


def hand_on(a, b, c, a_out, b_out, c_out):
    a_out[...] = a[...]
    b_out[...] = b[...]
    c_out[...] = c[...]


def solution(mesh):
    n, sections, replicas = mesh.shape["ctx"], mesh.shape["section"], mesh.shape["dp"]

    def shards(q, k, v, g, dots, frames, rows, source, wq, wp):
        tok, vis = k.shape[1], rows.shape[2]
        half = vis // 2
        width = GROUP * HEAD
        slots, quarter = source.shape[2], wp.shape[1] // 4
        anywhere = pl.BlockSpec(memory_space=pl.ANY)
        inside = pl.BlockSpec(memory_space=pltpu.VMEM)
        dma = pltpu.SemaphoreType.DMA
        model, side = wp.shape[0], wp.shape[1] // 2
        shapes = (
            jax.ShapeDtypeStruct(k.shape, BF),
            jax.ShapeDtypeStruct(v.shape, BF),
            jax.ShapeDtypeStruct((1, slots, quarter), BF),
        )
        outs = pl.pallas_call(
            functools.partial(kernel, n, sections, replicas),
            out_shape=shapes,
            in_specs=[anywhere] * 10,
            out_specs=(inside, inside, inside),
            scratch_shapes=[
                pltpu.VMEM((GROUP, 1, tok), F32),
                pltpu.VMEM(frames.shape, jnp.int32),
                pltpu.VMEM(rows.shape, jnp.int32),
                pltpu.VMEM(source.shape, jnp.int32),
                pltpu.VMEM((width, HEAD), BF),
                pltpu.VMEM((width, HEAD), BF),
                pltpu.VMEM((HEAD, width), BF),
                pltpu.VMEM((HEAD, width), BF),
                pltpu.VMEM((n, tok, HEAD), BF),
                pltpu.VMEM((n, tok, HEAD), BF),
                pltpu.VMEM((n, tok, width), F32),
                pltpu.VMEM((n, 2, tok, HEAD), BF),
                pltpu.VMEM((n, 2, tok, HEAD), BF),
                pltpu.VMEM((n, vis, tok), BF),
                pltpu.VMEM((n, vis, 2 * HEAD), BF),
                pltpu.VMEM((n, vis, 2 * HEAD), BF),
                pltpu.VMEM((model, wq.shape[0]), BF),
                pltpu.VMEM((model, side), BF),
                pltpu.VMEM((model, side), BF),
                pltpu.VMEM((1, width), F32),
                pltpu.VMEM((1, width), F32),
                pltpu.VMEM((HEAD, width), F32),
                pltpu.VMEM((sections, replicas * vis, width), BF),
                pltpu.VMEM((sections, replicas * vis, 2 * HEAD), BF),
                pltpu.VMEM((2, model, replicas * vis), BF),
                pltpu.VMEM((CHUNKS, replicas * vis, side // CHUNKS), BF),
                pltpu.VMEM((CHUNKS, sections, replicas, half, side // CHUNKS), BF),
                dma((8 + 2 * GROUP,)),
                dma((n,)), dma((n,)), dma((n,)), dma((n,)), dma((n,)), dma((n,)),
                dma((sections, replicas)), dma((sections, replicas)),
                dma((sections, replicas)), dma((sections, replicas)),
                dma((CHUNKS, sections, replicas)), dma((CHUNKS, sections, replicas)),
                dma((1,)), dma((1,)), dma((1,)), dma((1,)),
                dma((n,)), dma((n,)), dma((n,)), dma((n,)),
            ],
            compiler_params=pltpu.CompilerParams(
                collective_id=0, has_side_effects=True, vmem_limit_bytes=56 * 1024 * 1024
            ),
        )(q, k, v, g, dots.transpose(1, 0, 2), frames, rows, source, wq.T, wp)
        return pl.pallas_call(
            hand_on,
            out_shape=shapes,
            in_specs=[inside] * 3,
            out_specs=(inside,) * 3,
        )(*outs)

    placed = (
        P("dp", "ctx", "section"),
        P("dp", "ctx", "section"),
        P("dp", "ctx", "section"),
        P("dp", "ctx", "section"),
        P("dp", "section", "ctx"),
        P("dp", None),
        P("dp", "ctx", None),
        P("dp", ("ctx", "section"), None),
        P(None, ("section", "dp")),
        P(("section", "dp"), None),
    )
    return jax.shard_map(
        shards,
        mesh=mesh,
        in_specs=placed,
        out_specs=(
            P("dp", "ctx", "section"),
            P("dp", "ctx", "section"),
            P("dp", ("ctx", "section"), None),
        ),
        check_vma=False,
    )
```

```python
import functools
import math

import jax
import jax.numpy as jnp
from jax import lax
from jax.experimental import pallas as pl
from jax.experimental.pallas import tpu as pltpu
from jax.sharding import PartitionSpec as P

HEAD = 128
GROUP = 7
MASKED = -1e30
MESH = pl.DeviceIdType.MESH
CHUNKS = 2
BF = jnp.bfloat16
F32 = jnp.float32


def dot(a, b, over=(1, 0)):
    return lax.dot_general(a, b, (((over[0],), (over[1],)), ((), ())), preferred_element_type=F32)


def kernel(
    n, sections, replicas,
    q_in, k_in, v_in, g_in, dots_in, frames_in, rows_in, source_in, wq_in, wp_in,
    dk_out, dv_out, patch_out,
    dots, frames, rows, source, qs, gs, qst, gst, kbuf, vbuf, sbuf, gsend, grecv, hots, rsend, rrecv, wq, wp, swapped, top, total, gq_acc, gqsel, kvsel, gradbuf, psend, precv,
    load_sem, k_send, k_recv, v_send, v_recv, g_send, g_recv, a_send, a_recv, b_send, b_recv, p_send, p_recv, w_send, w_recv, s_send, s_recv, h_send, h_recv, r_send, r_recv,
):
    me = lax.axis_index("ctx")
    sec = lax.axis_index("section")
    rep = lax.axis_index("dp")
    tok = k_in.shape[1]
    vis = rows.shape[2]
    unrolled = n <= 8
    half = vis // 2
    width = GROUP * HEAD
    scale = 1.0 / math.sqrt(HEAD)
    factor = scale * math.log2(math.e)
    plane = [(a, b) for a in range(sections) for b in range(replicas) if a or b]

    def each(low, high, body):
        if n <= 8:
            for at in range(low, high):
                body(at)
        else:
            lax.fori_loop(low, high, lambda at, c: (body(at), c)[1], 0)

    def ahead(o):
        return {"ctx": lax.rem(me + o, n)}

    def behind(o):
        return {"ctx": lax.rem(me - o + n, n)}

    def peer(a, b):
        return {"section": lax.rem(sec + a, sections), "dp": lax.rem(rep + b, replicas)}

    def peer_back(a, b):
        return {"section": lax.rem(sec + a, sections), "dp": lax.rem(rep - b + replicas, replicas)}

    core = lax.rem(rep, 2)
    partner = {"dp": rep + 1 - 2 * core}
    columns = wp.shape[1] // CHUNKS

    def half_columns(which):
        return pl.ds(pl.multiple_of(which * wp.shape[1], wp.shape[1]), wp.shape[1])

    barrier = pltpu.get_barrier_semaphore()
    each(1, n, lambda o: pl.semaphore_signal(barrier, inc=1, device_id=ahead(o), device_id_type=MESH))
    for a, b in plane:
        pl.semaphore_signal(barrier, inc=1, device_id=peer(a, b), device_id_type=MESH)

    loads = [
        pltpu.make_async_copy(k_in.at[0], kbuf.at[0], load_sem.at[0]),
        pltpu.make_async_copy(v_in.at[0], vbuf.at[0], load_sem.at[1]),
        pltpu.make_async_copy(wq_in, wq, load_sem.at[2]),
        pltpu.make_async_copy(wp_in.at[:, half_columns(core)], wp, load_sem.at[3]),
    ]
    q_loads = [
        pltpu.make_async_copy(
            q_in.at[0, :, pl.ds(h * HEAD, HEAD)], qs.at[pl.ds(h * HEAD, HEAD), :], load_sem.at[4 + h]
        )
        for h in range(GROUP)
    ]
    g_loads = [
        pltpu.make_async_copy(
            g_in.at[0, :, pl.ds(h * HEAD, HEAD)], gs.at[pl.ds(h * HEAD, HEAD), :], load_sem.at[4 + GROUP + h]
        )
        for h in range(GROUP)
    ]
    small = [
        pltpu.make_async_copy(x, y, load_sem.at[4 + 2 * GROUP + i])
        for i, (x, y) in enumerate(((frames_in, frames), (rows_in, rows), (dots_in, dots), (source_in, source)))
    ]
    loads[0].start()
    for c in small:
        c.start()
    for c in q_loads:
        c.start()
    loads[1].start()
    for c in g_loads:
        c.start()
    loads[2].start()
    loads[3].start()
    pl.semaphore_wait(barrier, (n - 1) + len(plane))

    def remote(src, dst, send, recv, device):
        return pltpu.make_async_remote_copy(
            src_ref=src, dst_ref=dst, send_sem=send, recv_sem=recv, device_id=device, device_id_type=MESH
        )

    def k_copy(o):
        return remote(k_in.at[0], kbuf.at[o], k_send.at[o], k_recv.at[o], ahead(o))

    def v_copy(o):
        return remote(v_in.at[0], vbuf.at[o], v_send.at[o], v_recv.at[o], ahead(o))

    def g_copy(o):
        return remote(gsend.at[o], grecv.at[o], g_send.at[o], g_recv.at[o], behind(o))

    def h_copy(o):
        return remote(hots.at[0], hots.at[o], h_send.at[o], h_recv.at[o], ahead(o))

    def r_copy(o):
        return remote(rsend.at[o], rrecv.at[o], r_send.at[o], r_recv.at[o], behind(o))

    def pass_copy(a, b):
        at = pl.ds(pl.multiple_of(lax.rem(rep - b + replicas, replicas) * vis, vis), vis)
        return remote(gqsel.at[a, at], gqsel.at[a, at], a_send.at[a, b + 1], a_recv.at[a, b + 1], partner)

    across = [(a, b) for a, b in plane if b % 2 == 0]
    mine_at = pl.ds(pl.multiple_of(rep * vis, vis), vis)

    def sel_copy(buf, send, recv, a, b):
        return remote(buf.at[0, mine_at], buf.at[a, mine_at], send.at[a, b], recv.at[a, b], peer(a, b))

    def weight_copy():
        return remote(wp_in.at[:, half_columns(1 - core)], swapped, w_send.at[0], w_recv.at[0], partner)

    def grad_copy():
        return remote(gradbuf.at[0], gradbuf.at[1], s_send.at[0], s_recv.at[0], partner)

    def p_copy(i, a, b):
        first = lax.rem(rep - b + replicas, replicas) * vis + lax.rem(sec + a, sections) * half
        return remote(
            psend.at[i, pl.ds(pl.multiple_of(first, half), half)],
            precv.at[i, a, b],
            p_send.at[i, a, b],
            p_recv.at[i, a, b],
            peer_back(a, b),
        )

    each(1, n, lambda o: k_copy(o).start())
    each(1, n, lambda o: v_copy(o).start())
    weight_copy().start()

    for c in small:
        c.wait()
    query_frames = frames[:, pl.ds(pl.multiple_of(me * tok, tok), tok)]
    row_at = lax.broadcasted_iota(jnp.int32, (tok, tok), 0)
    col_at = lax.broadcasted_iota(jnp.int32, (tok, tok), 1)
    hot_t = (lax.broadcasted_iota(jnp.int32, (tok, vis), 0) == rows[0]).astype(F32).astype(BF)
    eye = (row_at == col_at).astype(F32).astype(BF)
    hot = dot(hot_t, eye, (0, 0)).astype(BF)
    hots[0] = hot
    each(1, n, lambda o: h_copy(o).start())
    dots_row = jnp.concatenate([dots[h] for h in range(GROUP)], axis=1)

    def bias_for(o):
        first = lax.rem(me - o + n, n) * tok
        line = frames[:, pl.ds(pl.multiple_of(first, tok), tok)].astype(F32)
        key_frames = jnp.transpose(jnp.broadcast_to(line, (tok, tok)))
        allowed = (first + row_at <= me * tok + col_at) | (key_frames == query_frames.astype(F32))
        return jnp.where(allowed, 0.0, MASKED)

    def wide(bias):
        return jnp.concatenate([bias] * GROUP, axis=1)

    top[...] = jnp.full_like(top, MASKED)
    total[...] = jnp.zeros_like(total)
    gq_acc[...] = jnp.zeros_like(gq_acc)

    def first_pass(o, s, bias):
        s = s + wide(bias)
        sbuf[o] = s
        top[...] = jnp.maximum(top[...], jnp.max(s, axis=0, keepdims=True))

    def first_remote(o):
        k_copy(o).wait_recv()
        first_pass(o, dot(kbuf[o], qst[...]), bias_for(o))

    biases = [bias_for(o) for o in range(n if unrolled else 1)]
    loads[0].wait()
    for h, c in enumerate(q_loads):
        c.wait()
        at = pl.ds(h * HEAD, HEAD)
        qst[:, at] = jnp.transpose(qs[at, :])
    first_pass(0, dot(kbuf[0], qst[...]), biases[0])
    for h, c in enumerate(g_loads):
        c.wait()
        at = pl.ds(h * HEAD, HEAD)
        gst[:, at] = jnp.transpose(gs[at, :])
    if unrolled:
        for o in range(1, n):
            k_copy(o).wait_recv()
        s = dot(kbuf[1:n].reshape((n - 1) * tok, HEAD), qst[...])
        for o in range(1, n):
            first_pass(o, s[(o - 1) * tok : o * tok], biases[o])
    else:
        lax.fori_loop(1, n, lambda o, c: (first_remote(o), c)[1], 0)

    def second_pass(o):
        e = jnp.exp2((sbuf[o] - top[...]) * factor)
        sbuf[o] = e
        total[...] += jnp.sum(e, axis=0, keepdims=True)

    each(0, n, second_pass)
    total[...] = 1.0 / total[...]

    loads[1].wait()

    def third_pass(p, values):
        gp = dot(values, gst[...])
        gsc = (p * (gp - dots_row)).astype(BF)
        return gsc, dot(gsc, qs[...]) * scale, dot(p.astype(BF), gs[...])

    def send_rows(o, gk, gv):
        gk, gv = gk.astype(BF), gv.astype(BF)
        gsend[o, 0] = gk
        gsend[o, 1] = gv
        rsend[o] = dot(hots[o], jnp.concatenate([gk, gv], axis=1)).astype(BF)
        r_copy(o).start()

    def third_remote(o):
        v_copy(o).wait_recv()
        h_copy(o).wait_recv()
        gsc, gk, gv = third_pass(sbuf[o] * total[...], vbuf[o])
        gq_acc[...] += dot(kbuf[o], gsc, (0, 0))
        send_rows(o, gk, gv)

    if unrolled:
        for o in range(1, n):
            v_copy(o).wait_recv()
            h_copy(o).wait_recv()
        keys, values = kbuf[...].reshape(n * tok, HEAD), vbuf[...].reshape(n * tok, HEAD)
        gsc, gk_all, gv_all = third_pass(sbuf[...].reshape(n * tok, width) * total[...], values)
        for o in range(1, n):
            send_rows(o, gk_all[o * tok : (o + 1) * tok], gv_all[o * tok : (o + 1) * tok])
        gk, gv = gk_all[0:tok], gv_all[0:tok]
        gq_acc[...] = dot(keys, gsc, (0, 0))
    else:
        lax.fori_loop(1, n, lambda o, c: (third_remote(o), c)[1], 0)
        gsc, gk, gv = third_pass(sbuf[0] * total[...], vbuf[0])
        gq_acc[...] += dot(kbuf[0], gsc, (0, 0))

    gq = (gq_acc[...] * scale).astype(BF)
    for h in range(GROUP):
        gqsel[0, mine_at, h * HEAD : (h + 1) * HEAD] = dot(
            hot, gq[:, h * HEAD : (h + 1) * HEAD], (1, 1)
        ).astype(BF)
    for a, b in across:
        sel_copy(gqsel, a_send, a_recv, a, b).start()
    pass_copy(0, 0).start()

    def picked(x):
        return lax.dot_general(
            hot.astype(F32), x, (((1,), (0,)), ((), ())),
            precision=lax.Precision.HIGHEST, preferred_element_type=F32,
        )

    def gather(copy, read, start):
        def step(o, pair):
            copy(o).wait_recv()
            x, y = read(o)
            return pair[0] + x.astype(F32), pair[1] + y.astype(F32)

        if n <= 8:
            for o in range(1, n):
                start = step(o, start)
            return start
        return lax.fori_loop(1, n, step, start)

    rows_k, rows_v = gather(
        r_copy, lambda o: (rrecv[o, :, 0:HEAD], rrecv[o, :, HEAD : 2 * HEAD]), (picked(gk), picked(gv))
    )
    kvsel[0, mine_at, 0:HEAD] = rows_k.astype(BF)
    kvsel[0, mine_at, HEAD : 2 * HEAD] = rows_v.astype(BF)
    for a, b in plane:
        sel_copy(kvsel, b_send, b_recv, a, b).start()
    for a, b in across:
        sel_copy(gqsel, a_send, a_recv, a, b).wait_recv()
        pass_copy(a, b).start()
    each(1, n, lambda o: g_copy(o).start())

    loads[2].wait()
    loads[3].wait()
    part = width + 2 * HEAD
    for a, b in [(0, 0)] + across:
        pass_copy(a, b).wait_recv()

    def weight_rows(a, offset, size):
        first = lax.rem(sec - a + sections, sections) * part + offset
        return wq[:, pl.ds(pl.multiple_of(first, HEAD), size)]

    grad = dot(weight_rows(0, 0, width), gqsel[0], (1, 1))
    for a in range(1, sections):
        grad = grad + dot(weight_rows(a, 0, width), gqsel[a], (1, 1))
    for a, b in plane:
        sel_copy(kvsel, b_send, b_recv, a, b).wait_recv()
    for a in range(sections):
        grad = grad + dot(weight_rows(a, width, 2 * HEAD), kvsel[a], (1, 1))
    gradbuf[0] = grad.astype(BF)
    grad_copy().start()
    own = dot(gradbuf[0], wp[...], (0, 0))
    weight_copy().wait_recv()
    grad_copy().wait_recv()
    other = jnp.transpose(gradbuf[1])
    for i in range(CHUNKS):
        at = slice(i * columns, (i + 1) * columns)
        psend[i] = (own[:, at] + dot(other, swapped[:, at])).astype(BF)
        for a, b in plane:
            p_copy(i, a, b).start()

    gk, gv = gather(g_copy, lambda o: (grecv[o, 0], grecv[o, 1]), (gk, gv))
    dk_out[0] = gk.astype(BF)
    dv_out[0] = gv.astype(BF)

    slots = source.shape[2]
    at = lax.broadcasted_iota(jnp.int32, (slots, slots), 0)
    slot_of = lax.rem(at, half) * 4 + lax.div(at, half)
    moved_t = (slot_of == source[0]).astype(F32).astype(BF)

    near, far = [], []
    for i in range(CHUNKS):
        even = psend[i, pl.ds(pl.multiple_of(rep * vis + sec * half, half), half), :].astype(F32)
        odd = jnp.zeros_like(even)
        for a, b in plane:
            p_copy(i, a, b).wait_recv()
            if b % 2:
                odd = odd + precv[i, a, b].astype(F32)
            else:
                even = even + precv[i, a, b].astype(F32)
        near.append(even)
        far.append(odd)
    first = [jnp.where(core == 0, x, y) for x, y in zip(near, far)]
    second = [jnp.where(core == 0, y, x) for x, y in zip(near, far)]
    pieces = first + second
    merged = jnp.concatenate(pieces, axis=0).astype(BF)
    patch_out[0] = dot(moved_t, merged, (0, 0)).astype(BF)

    each(1, n, lambda o: k_copy(o).wait_send())
    each(1, n, lambda o: v_copy(o).wait_send())
    each(1, n, lambda o: g_copy(o).wait_send())
    each(1, n, lambda o: h_copy(o).wait_send())
    each(1, n, lambda o: r_copy(o).wait_send())
    pass_copy(0, 0).wait_send()
    for a, b in across:
        sel_copy(gqsel, a_send, a_recv, a, b).wait_send()
        pass_copy(a, b).wait_send()
    weight_copy().wait_send()
    grad_copy().wait_send()
    for a, b in plane:
        sel_copy(kvsel, b_send, b_recv, a, b).wait_send()
        for i in range(CHUNKS):
            p_copy(i, a, b).wait_send()


def hand_on(a, b, c, a_out, b_out, c_out):
    a_out[...] = a[...]
    b_out[...] = b[...]
    c_out[...] = c[...]


def solution(mesh):
    n, sections, replicas = mesh.shape["ctx"], mesh.shape["section"], mesh.shape["dp"]

    def shards(q, k, v, g, dots, frames, rows, source, wq, wp):
        tok, vis = k.shape[1], rows.shape[2]
        half = vis // 2
        width = GROUP * HEAD
        slots, quarter = source.shape[2], wp.shape[1] // 4
        anywhere = pl.BlockSpec(memory_space=pl.ANY)
        inside = pl.BlockSpec(memory_space=pltpu.VMEM)
        dma = pltpu.SemaphoreType.DMA
        model, side = wp.shape[0], wp.shape[1] // 2
        shapes = (
            jax.ShapeDtypeStruct(k.shape, BF),
            jax.ShapeDtypeStruct(v.shape, BF),
            jax.ShapeDtypeStruct((1, slots, quarter), BF),
        )
        outs = pl.pallas_call(
            functools.partial(kernel, n, sections, replicas),
            out_shape=shapes,
            in_specs=[anywhere] * 10,
            out_specs=(inside, inside, inside),
            scratch_shapes=[
                pltpu.VMEM((GROUP, 1, tok), F32),
                pltpu.VMEM(frames.shape, jnp.int32),
                pltpu.VMEM(rows.shape, jnp.int32),
                pltpu.VMEM(source.shape, jnp.int32),
                pltpu.VMEM((width, HEAD), BF),
                pltpu.VMEM((width, HEAD), BF),
                pltpu.VMEM((HEAD, width), BF),
                pltpu.VMEM((HEAD, width), BF),
                pltpu.VMEM((n, tok, HEAD), BF),
                pltpu.VMEM((n, tok, HEAD), BF),
                pltpu.VMEM((n, tok, width), F32),
                pltpu.VMEM((n, 2, tok, HEAD), BF),
                pltpu.VMEM((n, 2, tok, HEAD), BF),
                pltpu.VMEM((n, vis, tok), BF),
                pltpu.VMEM((n, vis, 2 * HEAD), BF),
                pltpu.VMEM((n, vis, 2 * HEAD), BF),
                pltpu.VMEM((model, wq.shape[0]), BF),
                pltpu.VMEM((model, side), BF),
                pltpu.VMEM((model, side), BF),
                pltpu.VMEM((1, width), F32),
                pltpu.VMEM((1, width), F32),
                pltpu.VMEM((HEAD, width), F32),
                pltpu.VMEM((sections, replicas * vis, width), BF),
                pltpu.VMEM((sections, replicas * vis, 2 * HEAD), BF),
                pltpu.VMEM((2, model, replicas * vis), BF),
                pltpu.VMEM((CHUNKS, replicas * vis, side // CHUNKS), BF),
                pltpu.VMEM((CHUNKS, sections, replicas, half, side // CHUNKS), BF),
                dma((8 + 2 * GROUP,)),
                dma((n,)), dma((n,)), dma((n,)), dma((n,)), dma((n,)), dma((n,)),
                dma((sections, replicas)), dma((sections, replicas)),
                dma((sections, replicas)), dma((sections, replicas)),
                dma((CHUNKS, sections, replicas)), dma((CHUNKS, sections, replicas)),
                dma((1,)), dma((1,)), dma((1,)), dma((1,)),
                dma((n,)), dma((n,)), dma((n,)), dma((n,)),
            ],
            compiler_params=pltpu.CompilerParams(
                collective_id=0, has_side_effects=True, vmem_limit_bytes=56 * 1024 * 1024
            ),
        )(q, k, v, g, dots.transpose(1, 0, 2), frames, rows, source, wq.T, wp)
        return pl.pallas_call(
            hand_on,
            out_shape=shapes,
            in_specs=[inside] * 3,
            out_specs=(inside,) * 3,
        )(*outs)

    placed = (
        P("dp", "ctx", "section"),
        P("dp", "ctx", "section"),
        P("dp", "ctx", "section"),
        P("dp", "ctx", "section"),
        P("dp", "section", "ctx"),
        P("dp", None),
        P("dp", "ctx", None),
        P("dp", ("ctx", "section"), None),
        P(None, ("section", "dp")),
        P(("section", "dp"), None),
    )
    return jax.shard_map(
        shards,
        mesh=mesh,
        in_specs=placed,
        out_specs=(
            P("dp", "ctx", "section"),
            P("dp", "ctx", "section"),
            P("dp", ("ctx", "section"), None),
        ),
        check_vma=False,
    )
```
